512 devices in a mesh: frame: 64 (over y, x, z_hi), tok: 8 (over z_lo, core).
Axes of the slice: x: 4, y: 8, z: 8 (z_hi: 2, z_lo: 4; z = z_hi * 4 + z_lo), core: 2. Of those that a mesh axis runs over, the one named last changes fastest.
Arguments:
- queries: bfloat16 [64, 1024, 1024], P('frame', 'tok'), may hold values from -40 to 40
- key_rows: bfloat16 [64, 1024, 1024], P('frame', 'tok'), may hold values from -40 to 40
- value_rows: bfloat16 [64, 1024, 1024], P('frame', 'tok'), may hold values from -6 to 6
- grad_out: bfloat16 [64, 1024, 1024], P('frame', 'tok'), may hold values from -6 to 6
- video_of_frame: int32 [64], replicated, may hold values from 0 to 21, never falling along the last dimension, each value on 1 to 4 neighbouring positions
- age_pool: int32 [3], replicated, may hold values from 2 to 8, as said below
Outputs:
- attention_out: bfloat16 [64, 1024, 1024], P('frame', 'tok')
- grad_queries: bfloat16 [64, 1024, 1024], P('frame', 'tok')
- grad_keys: bfloat16 [64, 1024, 1024], P('frame', 'tok')
- grad_values: bfloat16 [64, 1024, 1024], P('frame', 'tok')
The draws below stay inside these ranges and needn't reach their ends.
Inputs may be any that keep to these rules, and one draw needn't show every extreme that they name: `video_of_frame`: video ids never fall along the frames; every video holds 1 to 4 frames. `age_pool`: each entry is 2, 4 or 8, and each of the three appears; entry a - 1 is the factor of a frame a frames older.
All inputs are finite; a program needn't handle non-finite values.
Results may differ from the reference program's by a relative error of at most 0.025.
Values may be sent and summed in bfloat16 or wider, within the bound.
A program may use at most 64 MiB of HBM per device.

```python
import math
import jax
import jax.numpy as jnp
import numpy as np
from jax import lax

HEADS = 16
HEAD = 64
HIST = 3
FRAME_TOKENS = 1024
FRAMES = 64
VIDEOS = 22


def paired_draw(key):
    columns = HEADS * HEAD
    shape = (FRAMES, FRAME_TOKENS, columns)
    query_draw = jnp.clip(jax.random.normal(jax.random.fold_in(key, 101), shape, jnp.float32), -6.0, 6.0)
    key_draw = jnp.clip(jax.random.normal(jax.random.fold_in(key, 102), shape, jnp.float32), -6.0, 6.0)
    return (query_draw, key_draw)


def draw_queries(key, part):
    return paired_draw(key)[0].astype(jnp.bfloat16)


def draw_key_rows(key, part):
    return paired_draw(key)[1].astype(jnp.bfloat16)


def draw_age_pool(key, part):
    cycle = (jnp.arange(HIST, dtype=jnp.int32) % 3 + 1).astype(jnp.int32)
    powers = jax.random.permutation(jax.random.fold_in(key, 201), cycle)
    return jnp.left_shift(jnp.ones((HIST,), jnp.int32), powers.astype(jnp.int32)).astype(jnp.int32)


def block_scale(stream_key, extent, cuts, low, high):
    level = 1.0
    for dim, parts in cuts:
        heights = jax.random.uniform(jax.random.fold_in(jax.random.fold_in(stream_key, 6), dim), (parts,), jnp.float32, low / len(cuts), high / len(cuts))
        level = level * jnp.repeat(jnp.exp(heights), extent[dim] // parts).reshape((-1,) + (1,) * (len(extent) - 1 - dim))
    return level


def split_up(amount, total, reach, slope):
    loads = [(1 << 20) // math.isqrt(grade ** slope) + 1 for grade in range(2, amount + 1)]
    rest, counts = total - reach - (amount - 1), [1] * (amount - 1)
    while rest > 0:
        free = [i for i in range(amount - 1) if counts[i] < reach]
        pool, left = sum([loads[i] for i in free]), rest
        for i in free:
            more = min(reach - counts[i], max(1, left * loads[i] // pool), rest)
            counts[i] = counts[i] + more
            rest = rest - more
    return np.array([reach] + counts)


def ragged_sizes(stream_key, amount, total, reach, lean):
    if amount == 2:
        one = jax.random.randint(stream_key, (), max(1, total - reach), min(reach, total - 1) + 1)
        return jnp.stack([one, total - one])
    tallies = jnp.asarray(split_up(amount, total, reach, lean), jnp.int32)
    pairs = (amount - 1) // 2
    giver, receiver = tallies[1:1 + 2 * pairs:2], tallies[2:2 + 2 * pairs:2]
    room = jnp.minimum(giver - 1, reach - receiver)
    shifted = jax.random.randint(jax.random.fold_in(stream_key, 1), (pairs,), 0, 1 << 20) % (room + 1)
    tallies = tallies.at[1:1 + 2 * pairs:2].set(giver - shifted).at[2:2 + 2 * pairs:2].set(receiver + shifted)
    return tallies[jax.random.permutation(jax.random.fold_in(stream_key, 2), amount)]


def noise(rng, dims, deviation, most, shards=(), kind=jnp.bfloat16):
    values = jax.random.normal(rng, dims, jnp.float32) * deviation
    if len(shards) > 0:
        values = block_scale(rng, dims, shards, -0.22, 0.18) * values
    return jnp.clip(values, min=-most, max=most).astype(kind)


def setup_inputs(seed: int = 0) -> dict:
    splits = jax.random.split(jax.random.key(seed), 7)
    return {
        "queries": draw_queries(jax.random.fold_in(splits[6], 71), 0),
        "key_rows": draw_key_rows(jax.random.fold_in(splits[6], 71), 0),
        "value_rows": noise(splits[2], (FRAMES, FRAME_TOKENS, HEADS * HEAD), 1.0, 6.0, ((0, 64), (1, 8))),
        "grad_out": noise(splits[3], (FRAMES, FRAME_TOKENS, HEADS * HEAD), 1.0, 6.0, ((0, 64), (1, 8))),
        "video_of_frame": jnp.searchsorted(jnp.cumsum(ragged_sizes(splits[4], VIDEOS, FRAMES, HIST + 1, 0)), jnp.arange(FRAMES), side="right").astype(jnp.int32),
        "age_pool": draw_age_pool(jax.random.fold_in(splits[6], 71), 0),
    }


def pooled_pick(source_rows, factor):
    total_rows, columns = source_rows.shape
    half_rows = total_rows // 2
    picked = jnp.zeros((half_rows, columns), jnp.float32)
    for stride in (2, 4, 8):
        average = source_rows.astype(jnp.float32).reshape(total_rows // stride, stride, columns).mean(axis=1)
        padded = jnp.pad(average, ((0, half_rows - total_rows // stride), (0, 0)))
        picked = jnp.where(factor == stride, padded, picked)
    return picked.astype(jnp.bfloat16)


def spread_back(pooled_grads, factor, total_rows):
    columns = pooled_grads.shape[1]
    widened = jnp.zeros((total_rows, columns), jnp.float32)
    for stride in (2, 4, 8):
        portion = pooled_grads[: total_rows // stride]
        spread = jnp.broadcast_to(portion[:, None, :], (total_rows // stride, stride, columns)).reshape(total_rows, columns) / stride
        widened = jnp.where(factor == stride, spread, widened)
    return widened


def attend_block(query_block, key_set, value_set, key_mask, grad_block, scaling):
    query_wide = query_block.astype(jnp.float32)
    key_wide = key_set.astype(jnp.float32)
    value_wide = value_set.astype(jnp.float32)
    grad_wide = grad_block.astype(jnp.float32)
    scores = jnp.einsum("qhd,khd->hqk", query_wide, key_wide) * scaling
    scores = jnp.where(key_mask[None, None, :], scores, -jnp.inf)
    highest = jnp.max(scores, axis=2, keepdims=True)
    exponent = jnp.exp(scores - highest)
    weights = exponent / jnp.sum(exponent, axis=2, keepdims=True)
    rounded = weights.astype(jnp.bfloat16)
    output = jnp.einsum("hqk,khd->qhd", rounded.astype(jnp.float32), value_wide).astype(jnp.bfloat16)
    inner_sum = jnp.sum(grad_wide * output.astype(jnp.float32), axis=2).T[:, :, None]
    grad_weights = jnp.einsum("qhd,khd->hqk", grad_wide, value_wide)
    grad_scores = (weights * (grad_weights - inner_sum)).astype(jnp.bfloat16)
    scores_wide = grad_scores.astype(jnp.float32)
    grad_query = jnp.einsum("hqk,khd->qhd", scores_wide, key_wide) * scaling
    grad_key_set = jnp.einsum("hqk,qhd->khd", scores_wide, query_wide) * scaling
    grad_value_set = jnp.einsum("hqk,qhd->khd", rounded.astype(jnp.float32), grad_wide)
    return output, grad_query, grad_key_set, grad_value_set


def reference(queries, key_rows, value_rows, grad_out, video_of_frame, age_pool):
    scaling = HEAD ** -0.5
    half_rows = FRAME_TOKENS // 2
    columns = HEADS * HEAD

    def frame_step(totals, frame_index):
        key_total, value_total = totals
        key_parts = [key_rows[frame_index]]
        value_parts = [value_rows[frame_index]]
        mask_parts = [jnp.ones((FRAME_TOKENS,), jnp.bool_)]
        sources = []
        for offset in range(1, HIST + 1):
            factor = age_pool[offset - 1]
            source = jnp.maximum(frame_index - offset, 0).astype(jnp.int32)
            usable = (frame_index >= offset) & (video_of_frame[source] == video_of_frame[frame_index])
            key_parts.append(pooled_pick(key_rows[source], factor))
            value_parts.append(pooled_pick(value_rows[source], factor))
            mask_parts.append(usable & (jnp.arange(half_rows) < FRAME_TOKENS // factor))
            sources.append(source)
        key_set = jnp.concatenate(key_parts, axis=0).reshape(-1, HEADS, HEAD)
        value_set = jnp.concatenate(value_parts, axis=0).reshape(-1, HEADS, HEAD)
        key_mask = jnp.concatenate(mask_parts)
        output, grad_query, grad_key_set, grad_value_set = attend_block(
            queries[frame_index].reshape(FRAME_TOKENS, HEADS, HEAD), key_set, value_set, key_mask,
            grad_out[frame_index].reshape(FRAME_TOKENS, HEADS, HEAD), scaling)
        grad_key_set = grad_key_set.reshape(-1, columns)
        grad_value_set = grad_value_set.reshape(-1, columns)
        key_total = key_total.at[frame_index].add(grad_key_set[:FRAME_TOKENS])
        value_total = value_total.at[frame_index].add(grad_value_set[:FRAME_TOKENS])
        for offset in range(1, HIST + 1):
            factor = age_pool[offset - 1]
            start_row = FRAME_TOKENS + (offset - 1) * half_rows
            key_total = key_total.at[sources[offset - 1]].add(spread_back(grad_key_set[start_row:start_row + half_rows], factor, FRAME_TOKENS))
            value_total = value_total.at[sources[offset - 1]].add(spread_back(grad_value_set[start_row:start_row + half_rows], factor, FRAME_TOKENS))
        return (key_total, value_total), (output.reshape(FRAME_TOKENS, columns), grad_query.reshape(FRAME_TOKENS, columns).astype(jnp.bfloat16))

    zero_grads = jnp.zeros((FRAMES, FRAME_TOKENS, columns), jnp.float32)
    (key_total, value_total), (attention_out, grad_queries) = lax.scan(frame_step, (zero_grads, zero_grads), jnp.arange(FRAMES, dtype=jnp.int32))
    return attention_out, grad_queries, key_total.astype(jnp.bfloat16), value_total.astype(jnp.bfloat16)
```

```python
import functools

import jax
import jax.numpy as jnp
from jax import lax
from jax.experimental import pallas as pl
from jax.experimental.pallas import tpu as pltpu
from jax.sharding import PartitionSpec as P

F32 = jnp.float32
BF16 = jnp.bfloat16
HEAD = 64
HIST = 3
PAIR = 2 * HEAD
BLOCK = 128
TOKENS = 1024
BLOCKS = TOKENS // BLOCK
HALF = TOKENS // 2
POOLED = TOKENS // 2 + TOKENS // 4 + TOKENS // 8
KEYS = TOKENS + POOLED
START = {2: 0, 4: TOKENS // 2, 8: TOKENS // 2 + TOKENS // 4}
CHAIN = 128
MESH = pl.DeviceIdType.MESH


def dot(a, b):
    return lax.dot_general(a, b, (((1,), (0,)), ((), ())), preferred_element_type=F32)


def dot_nt(a, b):
    return lax.dot_general(a, b, (((1,), (1,)), ((), ())), preferred_element_type=F32)


def pool_matrix(transposed):
    row = lax.broadcasted_iota(jnp.int32, (BLOCK, BLOCK), 1 if transposed else 0)
    col = lax.broadcasted_iota(jnp.int32, (BLOCK, BLOCK), 0 if transposed else 1)
    out = jnp.zeros((BLOCK, BLOCK), F32)
    base = 0
    for factor in (2, 4, 8):
        first = (row - base) * factor
        inside = (row >= base) & (row < base + BLOCK // factor)
        hit = inside & (col >= first) & (col < first + factor)
        out = jnp.where(hit, 1.0 / factor, out)
        base += BLOCK // factor
    return out.astype(BF16)


def pool_rows(rows, t, matrix, dst):
    pooled = dot(matrix, rows).astype(BF16)
    base = 0
    for factor in (2, 4, 8):
        size = BLOCK // factor
        dst[START[factor] + t * size : START[factor] + (t + 1) * size, :] = pooled[base : base + size]
        base += size


def by_age(factor, slots, dst):
    low = BLOCK
    dst[0:low, :] = jnp.where(
        factor == 2,
        slots[0:low, :],
        jnp.where(factor == 4, slots[START[4] : START[4] + low, :], slots[START[8] : START[8] + low, :]),
    )
    dst[low : 2 * low, :] = jnp.where(
        factor == 2, slots[low : 2 * low, :], slots[START[4] + low : START[4] + 2 * low, :]
    )
    dst[2 * low : HALF, :] = slots[2 * low : HALF, :]


def by_factor(factors, ages, dst, base):
    for factor in (2, 4, 8):
        size = TOKENS // factor
        dst[base + START[factor] : base + START[factor] + size, :] = jnp.where(
            factors[0] == factor,
            ages[0][0:size, :],
            jnp.where(factors[1] == factor, ages[1][0:size, :], ages[2][0:size, :]),
        )


def kernel(
    frames,
    video,
    age_pool,
    q_in,
    k_in,
    v_in,
    g_in,
    o_out,
    dq_out,
    dk_out,
    dv_out,
    q,
    g,
    kf,
    vf,
    kt,
    vt,
    s_buf,
    e_buf,
    ds_buf,
    qs_buf,
    gs_buf,
    pool_send,
    pool_recv,
    back_send,
    back_recv,
    slots,
    dk_sum,
    dv_sum,
    results,
    in_send,
    in_recv,
    pool_send_sem,
    pool_recv_sem,
    back_send_sem,
    back_recv_sem,
    out_send,
    out_recv,
):
    f = lax.axis_index("frame")
    t = lax.axis_index("tok")
    column, parity = f // 2, f % 2
    z, core = parity * 4 + t // 2, t % 2
    mine = column * 2 + core

    def at(column_, z_, core_):
        return (column_ * 2 + z_ // 4, (z_ % 4) * 2 + core_)

    def frame_at(frame_):
        return at(frame_ // 2, z, frame_ % 2)

    barrier = pltpu.get_barrier_semaphore()

    def greet(i, c):
        place = (z * 2 + core + i) % 16
        pl.semaphore_signal(
            barrier, inc=1, device_id=at(column, place // 2, place % 2), device_id_type=MESH
        )
        return c

    lax.fori_loop(1, 16, greet, 0)
    for a in range(1, HIST + 1):
        pl.semaphore_signal(
            barrier, inc=1, device_id=frame_at((mine + a) % frames), device_id_type=MESH
        )
        pl.semaphore_signal(
            barrier, inc=1, device_id=frame_at((mine + frames - a) % frames), device_id_type=MESH
        )
    pl.semaphore_wait(barrier, 15 + 2 * HIST)

    sources = (k_in, v_in, q_in, g_in)
    arrived = (kf, vf, q, g)
    my_rows = pl.ds(pl.multiple_of(t * BLOCK, BLOCK), BLOCK)

    def head_copy(n, zp):
        src = sources[n].at[0, :, pl.ds(pl.multiple_of(zp * PAIR, PAIR), PAIR)]
        dst = arrived[n].at[my_rows, :]
        remote = pltpu.make_async_remote_copy(
            src, dst, in_send.at[n, zp], in_recv.at[n, t], device_id=at(column, zp, parity), device_id_type=MESH
        )
        local = pltpu.make_async_copy(src, dst, in_recv.at[n, t])
        return remote, local, (zp == z) & (core == parity)

    def send_heads(n):
        def one(i, c):
            remote, local, here = head_copy(n, (z + 4 + i) % 8)

            @pl.when(here)
            def _():
                local.start()

            @pl.when(jnp.logical_not(here))
            def _():
                remote.start()

            return c

        lax.fori_loop(0, 8, one, 0)

    def heads_sent(n):
        def one(i, c):
            remote, _, here = head_copy(n, (z + 4 + i) % 8)

            @pl.when(jnp.logical_not(here))
            def _():
                remote.wait_send()

            return c

        lax.fori_loop(0, 8, one, 0)

    def wait_heads(n, block):
        part = arrived[n].at[pl.ds(pl.multiple_of(block * BLOCK, BLOCK), BLOCK), :]
        pltpu.make_async_copy(part, part, in_recv.at[n, block]).wait()

    for n in range(4):
        send_heads(n)

    factors = [age_pool[a] for a in range(HIST)]
    matrix = pool_matrix(False)

    def history(kv, a, back):
        src, dst, ss, rs = (
            (back_send, back_recv, back_send_sem, back_recv_sem)
            if back
            else (pool_send, pool_recv, pool_send_sem, pool_recv_sem)
        )
        other = (mine + frames - a) % frames if back else (mine + a) % frames
        return pltpu.make_async_remote_copy(
            src.at[kv, a - 1],
            dst.at[kv, a - 1],
            ss.at[kv, a - 1],
            rs.at[kv, a - 1],
            device_id=frame_at(other),
            device_id_type=MESH,
        )

    for kv, (rows, turned) in enumerate(((kf, kt), (vf, vt))):
        for block in range(BLOCKS):
            wait_heads(kv, block)
            pool_rows(rows[block * BLOCK : (block + 1) * BLOCK, :], block, matrix, slots)
        for a in range(1, HIST + 1):
            by_age(factors[a - 1], slots, pool_send.at[kv, a - 1])
            history(kv, a, False).start()
        turned[:, 0:TOKENS] = rows[0:TOKENS, :].T

    dead = {}
    for factor in (2, 4, 8):
        bias = jnp.float32(0.0)
        for a in range(1, HIST + 1):
            old = jnp.maximum(mine - a, 0)
            usable = (mine >= a) & (video[old] == video[mine])
            bias = jnp.where((factors[a - 1] == factor) & jnp.logical_not(usable), -1e30, bias)
        dead[factor] = bias

    for kv, (rows, turned) in enumerate(((kf, kt), (vf, vt))):
        for a in range(1, HIST + 1):
            history(kv, a, False).wait_recv()
        by_factor(factors, [pool_recv.at[kv, a] for a in range(HIST)], rows, TOKENS)
        turned[:, TOKENS:KEYS] = rows[TOKENS:KEYS, :].T

    outs = (o_out, dq_out, dk_out, dv_out)
    my_columns = pl.ds(pl.multiple_of(z * PAIR, PAIR), PAIR)

    def out_copy(n, block):
        src = results.at[n, pl.ds(pl.multiple_of(block * BLOCK, BLOCK), BLOCK), :]
        dst = outs[n].at[0, :, my_columns]
        remote = pltpu.make_async_remote_copy(
            src, dst, out_send.at[n, block], out_recv.at[n, z], device_id=(mine, block), device_id_type=MESH
        )
        local = pltpu.make_async_copy(src, dst, out_recv.at[n, z])
        return remote, local, (mine == f) & (block == t)

    def send_out(n, block):
        remote, local, here = out_copy(n, block)

        @pl.when(here)
        def _():
            local.start()

        @pl.when(jnp.logical_not(here))
        def _():
            remote.start()

    def bias_of(row):
        if row < TOKENS:
            return None
        row -= TOKENS
        return dead[2] if row < START[4] else dead[4] if row < START[8] else dead[8]

    def attend(b, c):
        wait_heads(2, b)
        wait_heads(3, b)
        rows = pl.ds(pl.multiple_of(b * BLOCK, BLOCK), BLOCK)
        top = lax.broadcasted_iota(jnp.int32, (PAIR, BLOCK), 0) < HEAD
        q_t = (q[rows, :].astype(F32) * HEAD**-0.5).T
        qs = jnp.concatenate([jnp.where(top, q_t, 0.0), jnp.where(top, 0.0, q_t)], axis=1).astype(BF16)
        qs_buf[b] = qs
        high = jnp.full((8, 2 * BLOCK), -jnp.inf, F32)
        for j in range(0, KEYS, CHAIN):
            s = dot(kf[j : j + CHAIN, :], qs)
            bias = bias_of(j)
            if bias is not None:
                s = s + bias
            s_buf[j : j + CHAIN, :] = s
            high = jnp.maximum(high, s.reshape(CHAIN // 8, 8, 2 * BLOCK).max(axis=0))
        high = high.max(axis=0, keepdims=True)
        total = jnp.zeros((8, 2 * BLOCK), F32)
        for j in range(0, KEYS, CHAIN):
            e = jnp.exp(s_buf[j : j + CHAIN, :] - high)
            total = total + e.reshape(CHAIN // 8, 8, 2 * BLOCK).sum(axis=0)
            e_buf[b, j : j + CHAIN, :] = e.astype(BF16)
        inverse = 1.0 / total.sum(axis=0, keepdims=True)
        both = dot(vt[...], e_buf[b]) * inverse
        o_t = jnp.where(top, both[:, :BLOCK], both[:, BLOCK:])
        o_round = o_t.astype(BF16).astype(F32)
        results[0, rows, :] = o_t.T.astype(BF16)
        send_out(0, b)
        g_t = g[rows, :].astype(F32).T
        gs = jnp.concatenate(
            [
                jnp.where(top, g_t, 0.0) * inverse[:, :BLOCK],
                jnp.where(top, 0.0, g_t) * inverse[:, BLOCK:],
            ],
            axis=1,
        ).astype(BF16)
        gs_buf[b] = gs
        inner = (gs.astype(F32) * jnp.concatenate([o_round, o_round], axis=1)).sum(axis=0, keepdims=True)
        for j in range(0, KEYS, CHAIN):
            dp = dot(vf[j : j + CHAIN, :], gs)
            ds = e_buf[b, j : j + CHAIN, :].astype(F32) * (dp - inner)
            ds_buf[b, j : j + CHAIN, :] = ds.astype(BF16)
        both = dot(kt[...], ds_buf[b])
        dq_t = jnp.where(top, both[:, :BLOCK], both[:, BLOCK:]) * HEAD**-0.5
        results[1, rows, :] = dq_t.T.astype(BF16)
        send_out(1, b)
        return c

    lax.fori_loop(0, BLOCKS, attend, 0)

    def set_grads(which, other, row, size):
        total = jnp.zeros((size, PAIR), F32)
        for b in range(BLOCKS):
            total = total + dot_nt(which[b, pl.ds(row, size), :], other[b])
        return total

    for kv, (which, other) in enumerate(((ds_buf, qs_buf), (e_buf, gs_buf))):

        def pooled_part(i, c):
            row = pl.multiple_of(i * BLOCK, BLOCK)
            slots[pl.ds(row, BLOCK), :] = set_grads(which, other, row + TOKENS, BLOCK).astype(BF16)
            return c

        lax.fori_loop(0, POOLED // BLOCK, pooled_part, 0)
        for a in range(1, HIST + 1):
            by_age(factors[a - 1], slots, back_send.at[kv, a - 1])
            history(kv, a, True).start()

    for which, other, dst in ((ds_buf, qs_buf, dk_sum), (e_buf, gs_buf, dv_sum)):

        def own_part(i, c):
            row = pl.multiple_of(i * 256, 256)
            dst[pl.ds(row, 256), :] = set_grads(which, other, row, 256)
            return c

        lax.fori_loop(0, TOKENS // 256, own_part, 0)

    spread = pool_matrix(True)
    for kv, total in enumerate((dk_sum, dv_sum)):
        for a in range(1, HIST + 1):
            history(kv, a, True).wait_recv()
        by_factor(factors, [back_recv.at[kv, a] for a in range(HIST)], slots, 0)
        for block in range(BLOCKS):
            pieces = [
                slots[START[p] + block * (BLOCK // p) : START[p] + (block + 1) * (BLOCK // p), :] for p in (2, 4, 8)
            ]
            pieces.append(jnp.zeros((BLOCK // 8, PAIR), BF16))
            rows = slice(block * BLOCK, (block + 1) * BLOCK)
            added = total[rows, :] + dot(spread, jnp.concatenate(pieces, axis=0))
            results[2 + kv, rows, :] = added.astype(BF16)
            send_out(2 + kv, block)

    for n in range(4):
        heads_sent(n)
    for kv in range(2):
        for a in range(1, HIST + 1):
            history(kv, a, False).wait_send()
            history(kv, a, True).wait_send()
    for n in range(4):

        def finish(i, c):
            remote, _, here = out_copy(n, i)

            @pl.when(jnp.logical_not(here))
            def _():
                remote.wait_send()

            part = outs[n].at[0, :, pl.ds(pl.multiple_of(i * PAIR, PAIR), PAIR)]
            pltpu.make_async_copy(part, part, out_recv.at[n, i]).wait()
            return c

        lax.fori_loop(0, 8, finish, 0)


def on_device(frames, queries, key_rows, value_rows, grad_out, video_of_frame, age_pool):
    vmem, dma = pltpu.VMEM, pltpu.SemaphoreType.DMA
    any_space = pl.BlockSpec(memory_space=pl.ANY)
    smem = pl.BlockSpec(memory_space=pltpu.SMEM)
    return pl.pallas_call(
        functools.partial(kernel, frames),
        out_shape=[jax.ShapeDtypeStruct(queries.shape, BF16)] * 4,
        in_specs=[smem, smem] + [any_space] * 4,
        out_specs=[any_space] * 4,
        scratch_shapes=[
            vmem((TOKENS, PAIR), BF16),
            vmem((TOKENS, PAIR), BF16),
            vmem((KEYS, PAIR), BF16),
            vmem((KEYS, PAIR), BF16),
            vmem((PAIR, KEYS), BF16),
            vmem((PAIR, KEYS), BF16),
            vmem((KEYS, 2 * BLOCK), F32),
            vmem((BLOCKS, KEYS, 2 * BLOCK), BF16),
            vmem((BLOCKS, KEYS, 2 * BLOCK), BF16),
            vmem((BLOCKS, PAIR, 2 * BLOCK), BF16),
            vmem((BLOCKS, PAIR, 2 * BLOCK), BF16),
            vmem((2, HIST, HALF, PAIR), BF16),
            vmem((2, HIST, HALF, PAIR), BF16),
            vmem((2, HIST, HALF, PAIR), BF16),
            vmem((2, HIST, HALF, PAIR), BF16),
            vmem((POOLED, PAIR), BF16),
            vmem((TOKENS, PAIR), F32),
            vmem((TOKENS, PAIR), F32),
            vmem((4, TOKENS, PAIR), BF16),
            dma((4, 8)),
            dma((4, 8)),
            dma((2, HIST)),
            dma((2, HIST)),
            dma((2, HIST)),
            dma((2, HIST)),
            dma((4, 8)),
            dma((4, 8)),
        ],
        compiler_params=pltpu.CompilerParams(
            collective_id=0, has_side_effects=True, vmem_limit_bytes=48 * 2**20
        ),
        cost_estimate=pl.CostEstimate(flops=5 * 2**29, bytes_accessed=2**21, transcendentals=2**22),
        name="attend_frames",
    )(video_of_frame, age_pool, queries, key_rows, value_rows, grad_out)


def solution(mesh):
    split = P("frame", "tok", None)
    return jax.shard_map(
        functools.partial(on_device, mesh.shape["frame"]),
        mesh=mesh,
        in_specs=(split,) * 4 + (P(), P()),
        out_specs=(split,) * 4,
        check_vma=False,
    )
```

```python
import functools

import jax
import jax.numpy as jnp
from jax import lax
from jax.experimental import pallas as pl
from jax.experimental.pallas import tpu as pltpu
from jax.sharding import PartitionSpec as P

F32 = jnp.float32
BF16 = jnp.bfloat16
HEAD = 64
HIST = 3
PAIR = 2 * HEAD
BLOCK = 128
TOKENS = 1024
BLOCKS = TOKENS // BLOCK
HALF = TOKENS // 2
POOLED = TOKENS // 2 + TOKENS // 4 + TOKENS // 8
KEYS = TOKENS + POOLED
START = {2: 0, 4: TOKENS // 2, 8: TOKENS // 2 + TOKENS // 4}
CHAIN = 128
VMEM_BYTES = 60 * 2**20
PART = BLOCK // 2
SPLIT = 2
MESH = pl.DeviceIdType.MESH


def dot(a, b):
    return lax.dot_general(a, b, (((1,), (0,)), ((), ())), preferred_element_type=F32)


def dot_nt(a, b):
    return lax.dot_general(a, b, (((1,), (1,)), ((), ())), preferred_element_type=F32)


def pool_matrix(factors, transposed):
    shape = (BLOCK, HIST * PART) if transposed else (HIST * PART, BLOCK)
    row = lax.broadcasted_iota(jnp.int32, shape, 1 if transposed else 0)
    token = lax.broadcasted_iota(jnp.int32, shape, 0 if transposed else 1)
    out = jnp.zeros(shape, F32)
    for a, factor in enumerate(factors):
        share = jnp.where(factor == 2, 0.5, jnp.where(factor == 4, 0.25, 0.125))
        first = (row - a * PART) * factor
        hit = (row >= a * PART) & (row < (a + 1) * PART) & (token >= first) & (token < first + factor)
        out = jnp.where(hit, share, out)
    return out.astype(BF16)


def by_age(factor, slots, dst, blocks):
    for b in blocks:
        two, four, eight = (START[p] + b * (BLOCK // p) for p in (2, 4, 8))
        low = PART // 4
        dst[b * PART : b * PART + low, :] = jnp.where(
            factor == 2,
            slots[two : two + low, :],
            jnp.where(factor == 4, slots[four : four + low, :], slots[eight : eight + low, :]),
        )
        dst[b * PART + low : b * PART + 2 * low, :] = jnp.where(
            factor == 2, slots[two + low : two + 2 * low, :], slots[four + low : four + 2 * low, :]
        )
        dst[b * PART + 2 * low : (b + 1) * PART, :] = slots[two + 2 * low : two + PART, :]


def by_factor(factors, ages, dst, base):
    for factor in (2, 4, 8):
        size = BLOCK // factor
        for b in range(BLOCKS):
            rows = slice(b * PART, b * PART + size)
            start = base + START[factor] + b * size
            dst[start : start + size, :] = jnp.where(
                factors[0] == factor,
                ages[0][rows, :],
                jnp.where(factors[1] == factor, ages[1][rows, :], ages[2][rows, :]),
            )


def kernel(
    frames,
    video,
    age_pool,
    q_in,
    k_in,
    v_in,
    g_in,
    o_out,
    dq_out,
    dk_out,
    dv_out,
    q,
    g,
    kf,
    vf,
    kt,
    vt,
    s_buf,
    e_buf,
    ds_buf,
    qs_buf,
    gs_buf,
    inverses,
    inners,
    pool_out,
    pool_in,
    back_out,
    back_in,
    slots,
    dk_sum,
    dv_sum,
    results,
    in_send,
    in_recv,
    pool_send,
    pool_recv,
    back_send,
    back_recv,
    out_send,
    out_recv,
):
    f = lax.axis_index("frame")
    t = lax.axis_index("tok")
    column, parity = f // 2, f % 2
    z, core = parity * 4 + t // 2, t % 2
    mine = column * 2 + core

    def at(column_, z_, core_):
        return (column_ * 2 + z_ // 4, (z_ % 4) * 2 + core_)

    def frame_at(frame_):
        return at(frame_ // 2, z, frame_ % 2)

    barrier = pltpu.get_barrier_semaphore()

    def greet(i, c):
        place = (z * 2 + core + i) % 16
        pl.semaphore_signal(
            barrier, inc=1, device_id=at(column, place // 2, place % 2), device_id_type=MESH
        )
        return c

    lax.fori_loop(1, 16, greet, 0)
    for a in range(1, HIST + 1):
        for other in ((mine + a) % frames, (mine + frames - a) % frames):
            pl.semaphore_signal(barrier, inc=1, device_id=frame_at(other), device_id_type=MESH)
    pl.semaphore_wait(barrier, 15 + 2 * HIST)

    sources = (k_in, v_in, q_in, g_in)
    arrived = (kf, vf, q, g)
    my_rows = pl.ds(pl.multiple_of(t * BLOCK, BLOCK), BLOCK)

    def rows_of(b):
        return pl.ds(pl.multiple_of(b * BLOCK, BLOCK), BLOCK)

    def head_copy(n, zp):
        src = sources[n].at[0, :, pl.ds(pl.multiple_of(zp * PAIR, PAIR), PAIR)]
        dst = arrived[n].at[my_rows, :]
        there = at(column, zp, parity)
        remote = pltpu.make_async_remote_copy(
            src, dst, in_send.at[n, zp], in_recv.at[n, t], device_id=there, device_id_type=MESH
        )
        local = pltpu.make_async_copy(src, dst, in_recv.at[n, t])
        return remote, local, (zp == z) & (core == parity)

    def send_heads(n):
        def one(i, c):
            remote, local, here = head_copy(n, (z + 4 + i) % 8)

            @pl.when(here)
            def _():
                local.start()

            @pl.when(jnp.logical_not(here))
            def _():
                remote.start()

            return c

        lax.fori_loop(0, 8, one, 0)

    def heads_sent(n):
        def one(i, c):
            remote, _, here = head_copy(n, i)

            @pl.when(jnp.logical_not(here))
            def _():
                remote.wait_send()

            return c

        lax.fori_loop(0, 8, one, 0)

    def wait_heads(n, b):
        part = arrived[n].at[rows_of(b), :]
        pltpu.make_async_copy(part, part, in_recv.at[n, b]).wait()

    for n in range(4):
        send_heads(n)

    factors = [age_pool[a] for a in range(HIST)]
    matrix = pool_matrix(factors, False)
    sets = ((kf, kt), (vf, vt))

    def history(kv, a, part, back=False):
        src, dst, ss, rs = (
            (back_out, back_in, back_send, back_recv) if back else (pool_out, pool_in, pool_send, pool_recv)
        )
        rows = slice(part * HALF // SPLIT, (part + 1) * HALF // SPLIT)
        other = (mine + frames - a) % frames if back else (mine + a) % frames
        return pltpu.make_async_remote_copy(
            src.at[kv, a - 1, rows],
            dst.at[kv, a - 1, rows],
            ss.at[kv, a - 1, part],
            rs.at[kv, a - 1, part],
            device_id=frame_at(other),
            device_id_type=MESH,
        )

    def pool(kv):
        rows, turned = sets[kv]
        for part in range(SPLIT):
            for b in range(part * BLOCKS // SPLIT, (part + 1) * BLOCKS // SPLIT):
                wait_heads(kv, b)
                means = dot(matrix, rows[b * BLOCK : (b + 1) * BLOCK, :]).astype(BF16)
                for a in range(HIST):
                    pool_out[kv, a, b * PART : (b + 1) * PART, :] = means[a * PART : (a + 1) * PART]
            for a in range(1, HIST + 1):
                history(kv, a, part).start()
        turned[:, 0:TOKENS] = rows[0:TOKENS, :].T

    def history_here(kv):
        rows, turned = sets[kv]
        for part in range(SPLIT):
            for a in range(1, HIST + 1):
                history(kv, a, part).wait_recv()
        by_factor(factors, [pool_in.at[kv, a] for a in range(HIST)], rows, TOKENS)
        turned[:, TOKENS:KEYS] = rows[TOKENS:KEYS, :].T

    dead = {}
    for factor in (2, 4, 8):
        bias = jnp.float32(0.0)
        for a in range(1, HIST + 1):
            old = jnp.maximum(mine - a, 0)
            usable = (mine >= a) & (video[old] == video[mine])
            bias = jnp.where((factors[a - 1] == factor) & jnp.logical_not(usable), -1e30, bias)
        dead[factor] = bias

    outs = (o_out, dq_out, dk_out, dv_out)
    my_columns = pl.ds(pl.multiple_of(z * PAIR, PAIR), PAIR)

    def out_copy(n, b):
        src = results.at[n, rows_of(b), :]
        dst = outs[n].at[0, :, my_columns]
        remote = pltpu.make_async_remote_copy(
            src, dst, out_send.at[n, b], out_recv.at[n, z], device_id=(mine, b), device_id_type=MESH
        )
        local = pltpu.make_async_copy(src, dst, out_recv.at[n, z])
        return remote, local, (mine == f) & (b == t)

    def send_out(n, b):
        remote, local, here = out_copy(n, b)

        @pl.when(here)
        def _():
            local.start()

        @pl.when(jnp.logical_not(here))
        def _():
            remote.start()

    top = lax.broadcasted_iota(jnp.int32, (PAIR, BLOCK), 0) < HEAD

    def bias_of(row):
        if row < TOKENS:
            return None
        row -= TOKENS
        return dead[2] if row < START[4] else dead[4] if row < START[8] else dead[8]

    def scores(b, slot):
        q_t = (q[rows_of(b), :].astype(F32) * HEAD**-0.5).T
        qs = jnp.concatenate([jnp.where(top, q_t, 0.0), jnp.where(top, 0.0, q_t)], axis=1).astype(BF16)
        qs_buf[b] = qs
        high = jnp.full((8, 2 * BLOCK), -jnp.inf, F32)
        for j in range(0, KEYS, CHAIN):
            s = dot(kf[j : j + CHAIN, :], qs)
            bias = bias_of(j)
            if bias is not None:
                s = s + bias
            s_buf[slot, j : j + CHAIN, :] = s
            high = jnp.maximum(high, s.reshape(CHAIN // 8, 8, 2 * BLOCK).max(axis=0))
        return high.max(axis=0, keepdims=True)

    def exponents(b, slot, high):
        total = jnp.zeros((8, 2 * BLOCK), F32)
        for j in range(0, KEYS, CHAIN):
            e = jnp.exp(s_buf[slot, j : j + CHAIN, :] - high)
            total = total + e.reshape(CHAIN // 8, 8, 2 * BLOCK).sum(axis=0)
            e_buf[b, j : j + CHAIN, :] = e.astype(BF16)
        inverses[b] = jnp.broadcast_to(1.0 / total.sum(axis=0, keepdims=True), (8, 2 * BLOCK))

    def scaled_grads(b, c):
        wait_heads(3, b)
        inverse = inverses[b][0:1, :]
        g_t = g[rows_of(b), :].astype(F32).T
        gs_buf[b] = jnp.concatenate(
            [
                jnp.where(top, g_t, 0.0) * inverse[:, :BLOCK],
                jnp.where(top, 0.0, g_t) * inverse[:, BLOCK:],
            ],
            axis=1,
        ).astype(BF16)
        return c

    def attend(b, c):
        both = dot(vt[...], e_buf[b]) * inverses[b][0:1, :]
        o_t = jnp.where(top, both[:, :BLOCK], both[:, BLOCK:])
        o_round = o_t.astype(BF16).astype(F32)
        results[0, rows_of(b), :] = o_t.T.astype(BF16)
        send_out(0, b)
        gs = gs_buf[b].astype(F32)
        inner = (gs * jnp.concatenate([o_round, o_round], axis=1)).sum(axis=0, keepdims=True)
        inners[b] = jnp.broadcast_to(inner, (8, 2 * BLOCK))
        return c

    def score_grads(b, low, high):
        gs, inner = gs_buf[b], inners[b][0:1, :]
        for j in range(low, high, CHAIN):
            dp = dot(vf[j : j + CHAIN, :], gs)
            ds = e_buf[b, j : j + CHAIN, :].astype(F32) * (dp - inner)
            ds_buf[b, j : j + CHAIN, :] = ds.astype(BF16)

    def query_grads(b):
        both = dot(kt[...], ds_buf[b])
        dq_t = jnp.where(top, both[:, :BLOCK], both[:, BLOCK:]) * HEAD**-0.5
        results[1, rows_of(b), :] = dq_t.T.astype(BF16)
        send_out(1, b)

    def set_grads(which, other, row, size):
        total = jnp.zeros((size, PAIR), F32)
        for b in range(BLOCKS):
            total = total + dot_nt(which[b, row : row + size, :], other[b])
        return total

    def pooled_part(kv, which, other):
        for row in range(0, POOLED, POOLED // 2):
            part = set_grads(which, other, TOKENS + row, POOLED // 2)
            slots[row : row + POOLED // 2, :] = part.astype(BF16)
        for part in range(SPLIT):
            for a in range(1, HIST + 1):
                blocks = range(part * BLOCKS // SPLIT, (part + 1) * BLOCKS // SPLIT)
                by_age(factors[a - 1], slots, back_out.at[kv, a - 1], blocks)
                history(kv, a, part, True).start()

    def own_part(which, other, dst):
        for row in range(0, TOKENS, HALF):
            dst[row : row + HALF, :] = set_grads(which, other, row, HALF)

    spread = pool_matrix(factors, True)

    def finish_set(kv, total):
        for part in range(SPLIT):
            for a in range(1, HIST + 1):
                history(kv, a, part, True).wait_recv()
            for b in range(part * BLOCKS // SPLIT, (part + 1) * BLOCKS // SPLIT):
                pieces = [back_in[kv, a, b * PART : (b + 1) * PART, :] for a in range(HIST)]
                rows = slice(b * BLOCK, (b + 1) * BLOCK)
                added = total[rows, :] + dot(spread, jnp.concatenate(pieces, axis=0))
                results[2 + kv, rows, :] = added.astype(BF16)
                send_out(2 + kv, b)

    pool(0)
    pool(1)
    history_here(0)
    for b in range(BLOCKS):
        wait_heads(2, b)
    high0 = scores(0, 0)

    def two_blocks(i, high0):
        b = 2 * i
        high1 = scores(b + 1, 1)
        exponents(b, 0, high0)
        high2 = scores(b + 2, 0)
        exponents(b + 1, 1, high1)
        return high2

    high6 = lax.fori_loop(0, BLOCKS // 2 - 1, two_blocks, high0)
    high7 = scores(BLOCKS - 1, 1)
    exponents(BLOCKS - 2, 0, high6)
    exponents(BLOCKS - 1, 1, high7)
    lax.fori_loop(0, BLOCKS, scaled_grads, 0)
    pooled_part(1, e_buf, gs_buf)
    own_part(e_buf, gs_buf, dv_sum)
    history_here(1)
    lax.fori_loop(0, BLOCKS, attend, 0)

    def old_scores(b, c):
        score_grads(b, TOKENS, KEYS)
        return c

    lax.fori_loop(0, BLOCKS, old_scores, 0)
    pooled_part(0, ds_buf, qs_buf)

    def own_scores(b, c):
        score_grads(b, 0, TOKENS)
        query_grads(b)
        return c

    lax.fori_loop(0, BLOCKS, own_scores, 0)
    finish_set(1, dv_sum)
    own_part(ds_buf, qs_buf, dk_sum)
    finish_set(0, dk_sum)

    for n in range(4):
        heads_sent(n)
    for kv in range(2):
        for a in range(1, HIST + 1):
            for part in range(SPLIT):
                history(kv, a, part).wait_send()
                history(kv, a, part, True).wait_send()
    for n in (0, 1, 3, 2):

        def finish(i, c):
            remote, _, here = out_copy(n, i)

            @pl.when(jnp.logical_not(here))
            def _():
                remote.wait_send()

            part = outs[n].at[0, :, pl.ds(pl.multiple_of(i * PAIR, PAIR), PAIR)]
            pltpu.make_async_copy(part, part, out_recv.at[n, i]).wait()
            return c

        lax.fori_loop(0, 8, finish, 0)


def on_device(frames, queries, key_rows, value_rows, grad_out, video_of_frame, age_pool):
    vmem, dma = pltpu.VMEM, pltpu.SemaphoreType.DMA
    any_space = pl.BlockSpec(memory_space=pl.ANY)
    smem = pl.BlockSpec(memory_space=pltpu.SMEM)
    return pl.pallas_call(
        functools.partial(kernel, frames),
        out_shape=[jax.ShapeDtypeStruct(queries.shape, BF16)] * 4,
        in_specs=[smem, smem] + [any_space] * 4,
        out_specs=[any_space] * 4,
        scratch_shapes=[
            vmem((TOKENS, PAIR), BF16),
            vmem((TOKENS, PAIR), BF16),
            vmem((KEYS, PAIR), BF16),
            vmem((KEYS, PAIR), BF16),
            vmem((PAIR, KEYS), BF16),
            vmem((PAIR, KEYS), BF16),
            vmem((2, KEYS, 2 * BLOCK), F32),
            vmem((BLOCKS, KEYS, 2 * BLOCK), BF16),
            vmem((BLOCKS, KEYS, 2 * BLOCK), BF16),
            vmem((BLOCKS, PAIR, 2 * BLOCK), BF16),
            vmem((BLOCKS, PAIR, 2 * BLOCK), BF16),
            vmem((BLOCKS, 8, 2 * BLOCK), F32),
            vmem((BLOCKS, 8, 2 * BLOCK), F32),
            vmem((2, HIST, HALF, PAIR), BF16),
            vmem((2, HIST, HALF, PAIR), BF16),
            vmem((2, HIST, HALF, PAIR), BF16),
            vmem((2, HIST, HALF, PAIR), BF16),
            vmem((POOLED, PAIR), BF16),
            vmem((TOKENS, PAIR), F32),
            vmem((TOKENS, PAIR), F32),
            vmem((4, TOKENS, PAIR), BF16),
            dma((4, 8)),
            dma((4, 8)),
            dma((2, HIST, SPLIT)),
            dma((2, HIST, SPLIT)),
            dma((2, HIST, SPLIT)),
            dma((2, HIST, SPLIT)),
            dma((4, 8)),
            dma((4, 8)),
        ],
        compiler_params=pltpu.CompilerParams(
            collective_id=0, has_side_effects=True, vmem_limit_bytes=VMEM_BYTES
        ),
        cost_estimate=pl.CostEstimate(flops=5 * 2**29, bytes_accessed=2**21, transcendentals=2**22),
        name="attend_frames",
    )(video_of_frame, age_pool, queries, key_rows, value_rows, grad_out)


def solution(mesh):
    split = P("frame", "tok", None)
    return jax.shard_map(
        functools.partial(on_device, mesh.shape["frame"]),
        mesh=mesh,
        in_specs=(split,) * 4 + (P(), P()),
        out_specs=(split,) * 4,
        check_vma=False,
    )
```

```python
import functools

import jax
import jax.numpy as jnp
from jax import lax
from jax.experimental import pallas as pl
from jax.experimental.pallas import tpu as pltpu
from jax.sharding import PartitionSpec as P

F32 = jnp.float32
BF16 = jnp.bfloat16
HEAD = 64
HIST = 3
PAIR = 2 * HEAD
BLOCK = 128
TOKENS = 1024
BLOCKS = TOKENS // BLOCK
HALF = TOKENS // 2
POOLED = TOKENS // 2 + TOKENS // 4 + TOKENS // 8
KEYS = TOKENS + POOLED
START = {2: 0, 4: TOKENS // 2, 8: TOKENS // 2 + TOKENS // 4}
CHAIN = 128
VMEM_BYTES = 60 * 2**20
PART = BLOCK // 2
SPLIT = 2
MESH = pl.DeviceIdType.MESH


def dot(a, b):
    return lax.dot_general(a, b, (((1,), (0,)), ((), ())), preferred_element_type=F32)


def dot_nt(a, b):
    return lax.dot_general(a, b, (((1,), (1,)), ((), ())), preferred_element_type=F32)


def pool_matrix(factors, transposed):
    shape = (BLOCK, HIST * PART) if transposed else (HIST * PART, BLOCK)
    row = lax.broadcasted_iota(jnp.int32, shape, 1 if transposed else 0)
    token = lax.broadcasted_iota(jnp.int32, shape, 0 if transposed else 1)
    out = jnp.zeros(shape, F32)
    for a, factor in enumerate(factors):
        share = jnp.where(factor == 2, 0.5, jnp.where(factor == 4, 0.25, 0.125))
        first = (row - a * PART) * factor
        hit = (row >= a * PART) & (row < (a + 1) * PART) & (token >= first) & (token < first + factor)
        out = jnp.where(hit, share, out)
    return out.astype(BF16)


def by_age(factor, slots, dst, blocks):
    for b in blocks:
        two, four, eight = (START[p] + b * (BLOCK // p) for p in (2, 4, 8))
        low = PART // 4
        dst[b * PART : b * PART + low, :] = jnp.where(
            factor == 2,
            slots[two : two + low, :],
            jnp.where(factor == 4, slots[four : four + low, :], slots[eight : eight + low, :]),
        )
        dst[b * PART + low : b * PART + 2 * low, :] = jnp.where(
            factor == 2, slots[two + low : two + 2 * low, :], slots[four + low : four + 2 * low, :]
        )
        dst[b * PART + 2 * low : (b + 1) * PART, :] = slots[two + 2 * low : two + PART, :]


def by_factor(factors, ages, dst, base):
    for factor in (2, 4, 8):
        size = BLOCK // factor
        for b in range(BLOCKS):
            rows = slice(b * PART, b * PART + size)
            start = base + START[factor] + b * size
            dst[start : start + size, :] = jnp.where(
                factors[0] == factor,
                ages[0][rows, :],
                jnp.where(factors[1] == factor, ages[1][rows, :], ages[2][rows, :]),
            )


def kernel(
    frames,
    video,
    age_pool,
    q_in,
    k_in,
    v_in,
    g_in,
    o_out,
    dq_out,
    dk_out,
    dv_out,
    q,
    g,
    kf,
    vf,
    kt,
    vt,
    s_buf,
    e_buf,
    ds_buf,
    qs_buf,
    gs_buf,
    inverses,
    inners,
    pool_out,
    pool_in,
    back_out,
    back_in,
    slots,
    o_own,
    dk_sum,
    dv_sum,
    results,
    in_send,
    in_recv,
    pool_send,
    pool_recv,
    back_send,
    back_recv,
    out_send,
    out_recv,
):
    f = lax.axis_index("frame")
    t = lax.axis_index("tok")
    column, parity = f // 2, f % 2
    z, core = parity * 4 + t // 2, t % 2
    mine = column * 2 + core

    def at(column_, z_, core_):
        return (column_ * 2 + z_ // 4, (z_ % 4) * 2 + core_)

    def frame_at(frame_):
        return at(frame_ // 2, z, frame_ % 2)

    barrier = pltpu.get_barrier_semaphore()

    def greet(i, c):
        place = (z * 2 + core + i) % 16
        pl.semaphore_signal(
            barrier, inc=1, device_id=at(column, place // 2, place % 2), device_id_type=MESH
        )
        return c

    lax.fori_loop(1, 16, greet, 0)
    for a in range(1, HIST + 1):
        for other in ((mine + a) % frames, (mine + frames - a) % frames):
            pl.semaphore_signal(barrier, inc=1, device_id=frame_at(other), device_id_type=MESH)
    pl.semaphore_wait(barrier, 15 + 2 * HIST)

    sources = (k_in, v_in, q_in, g_in)
    arrived = (kf, vf, q, g)
    my_rows = pl.ds(pl.multiple_of(t * BLOCK, BLOCK), BLOCK)

    def rows_of(b):
        return pl.ds(pl.multiple_of(b * BLOCK, BLOCK), BLOCK)

    def head_copy(n, zp):
        src = sources[n].at[0, :, pl.ds(pl.multiple_of(zp * PAIR, PAIR), PAIR)]
        dst = arrived[n].at[my_rows, :]
        there = at(column, zp, parity)
        remote = pltpu.make_async_remote_copy(
            src, dst, in_send.at[n, zp], in_recv.at[n, t], device_id=there, device_id_type=MESH
        )
        local = pltpu.make_async_copy(src, dst, in_recv.at[n, t])
        return remote, local, (zp == z) & (core == parity)

    def send_heads(n):
        def one(i, c):
            remote, local, here = head_copy(n, (z + 12 + (1 - 2 * (i % 2)) * ((i + 1) // 2)) % 8)

            @pl.when(here)
            def _():
                local.start()

            @pl.when(jnp.logical_not(here))
            def _():
                remote.start()

            return c

        lax.fori_loop(0, 8, one, 0)

    def heads_sent(n):
        def one(i, c):
            remote, _, here = head_copy(n, i)

            @pl.when(jnp.logical_not(here))
            def _():
                remote.wait_send()

            return c

        lax.fori_loop(0, 8, one, 0)

    def wait_heads(n, b):
        part = arrived[n].at[rows_of(b), :]
        pltpu.make_async_copy(part, part, in_recv.at[n, b]).wait()

    for n in range(4):
        send_heads(n)

    facing = (z + 4) % 8
    first = jnp.where(facing // 4 == core, facing % 4, 3)

    def nth(n):
        return ((first + 4 - n // 2) % 4) * 2 + n % 2

    factors = [age_pool[a] for a in range(HIST)]
    matrix = pool_matrix(factors, False)
    sets = ((kf, kt), (vf, vt))

    def history(kv, a, part, back=False):
        src, dst, ss, rs = (
            (back_out, back_in, back_send, back_recv) if back else (pool_out, pool_in, pool_send, pool_recv)
        )
        rows = slice(part * HALF // SPLIT, (part + 1) * HALF // SPLIT)
        other = (mine + frames - a) % frames if back else (mine + a) % frames
        return pltpu.make_async_remote_copy(
            src.at[kv, a - 1, rows],
            dst.at[kv, a - 1, rows],
            ss.at[kv, a - 1, part],
            rs.at[kv, a - 1, part],
            device_id=frame_at(other),
            device_id_type=MESH,
        )

    def pool(kv):
        rows, turned = sets[kv]
        for part in range(SPLIT):
            for b in range(part * BLOCKS // SPLIT, (part + 1) * BLOCKS // SPLIT):
                wait_heads(kv, b)
                means = dot(matrix, rows[b * BLOCK : (b + 1) * BLOCK, :]).astype(BF16)
                for a in range(HIST):
                    pool_out[kv, a, b * PART : (b + 1) * PART, :] = means[a * PART : (a + 1) * PART]
            for a in range(1, HIST + 1):
                history(kv, a, part).start()
        turned[:, 0:TOKENS] = rows[0:TOKENS, :].T

    def history_here(kv):
        rows, turned = sets[kv]
        for part in range(SPLIT):
            for a in range(1, HIST + 1):
                history(kv, a, part).wait_recv()
        by_factor(factors, [pool_in.at[kv, a] for a in range(HIST)], rows, TOKENS)
        turned[:, TOKENS:KEYS] = rows[TOKENS:KEYS, :].T

    dead = {}
    for factor in (2, 4, 8):
        bias = jnp.float32(0.0)
        for a in range(1, HIST + 1):
            old = jnp.maximum(mine - a, 0)
            usable = (mine >= a) & (video[old] == video[mine])
            bias = jnp.where((factors[a - 1] == factor) & jnp.logical_not(usable), -1e30, bias)
        dead[factor] = bias

    outs = (o_out, dq_out, dk_out, dv_out)
    my_columns = pl.ds(pl.multiple_of(z * PAIR, PAIR), PAIR)

    def out_copy(n, b):
        src = results.at[n, rows_of(b), :]
        dst = outs[n].at[0, :, my_columns]
        remote = pltpu.make_async_remote_copy(
            src, dst, out_send.at[n, b], out_recv.at[n, z], device_id=(mine, b), device_id_type=MESH
        )
        local = pltpu.make_async_copy(src, dst, out_recv.at[n, z])
        return remote, local, (mine == f) & (b == t)

    def send_out(n, b):
        remote, local, here = out_copy(n, b)

        @pl.when(here)
        def _():
            local.start()

        @pl.when(jnp.logical_not(here))
        def _():
            remote.start()

    top = lax.broadcasted_iota(jnp.int32, (PAIR, BLOCK), 0) < HEAD

    def bias_of(row):
        if row < TOKENS:
            return None
        row -= TOKENS
        return dead[2] if row < START[4] else dead[4] if row < START[8] else dead[8]

    def scores(n, slot):
        b = nth(n)
        wait_heads(2, b)
        q_t = (q[rows_of(b), :].astype(F32) * HEAD**-0.5).T
        qs = jnp.concatenate([jnp.where(top, q_t, 0.0), jnp.where(top, 0.0, q_t)], axis=1).astype(BF16)
        qs_buf[b] = qs
        high = jnp.full((8, 2 * BLOCK), -jnp.inf, F32)
        for j in range(0, KEYS, CHAIN):
            s = dot(kf[j : j + CHAIN, :], qs)
            bias = bias_of(j)
            if bias is not None:
                s = s + bias
            s_buf[slot, j : j + CHAIN, :] = s
            high = jnp.maximum(high, s.reshape(CHAIN // 8, 8, 2 * BLOCK).max(axis=0))
        return high.max(axis=0, keepdims=True)

    def exponents(n, slot, high):
        b = nth(n)
        total = jnp.zeros((8, 2 * BLOCK), F32)
        for j in range(0, KEYS, CHAIN):
            e = jnp.exp(s_buf[slot, j : j + CHAIN, :] - high)
            total = total + e.reshape(CHAIN // 8, 8, 2 * BLOCK).sum(axis=0)
            e_buf[b, j : j + CHAIN, :] = e.astype(BF16)
        inverses[b] = jnp.broadcast_to(1.0 / total.sum(axis=0, keepdims=True), (8, 2 * BLOCK))

    def own_output(b, c):
        o_own[b] = dot(vt[:, 0:TOKENS], e_buf[b, 0:TOKENS, :])
        return c

    def scaled_grads(n, c):
        b = nth(n)
        wait_heads(3, b)
        inverse = inverses[b][0:1, :]
        g_t = g[rows_of(b), :].astype(F32).T
        gs_buf[b] = jnp.concatenate(
            [
                jnp.where(top, g_t, 0.0) * inverse[:, :BLOCK],
                jnp.where(top, 0.0, g_t) * inverse[:, BLOCK:],
            ],
            axis=1,
        ).astype(BF16)
        return c

    def turn(n):
        return ((z + n // 2) % 4) * 2 + n % 2

    def attend(n, c):
        b = turn(n)
        both = o_own[b] + dot(vt[:, TOKENS:KEYS], e_buf[b, TOKENS:KEYS, :])
        both = both * inverses[b][0:1, :]
        o_t = jnp.where(top, both[:, :BLOCK], both[:, BLOCK:])
        o_round = o_t.astype(BF16).astype(F32)
        results[0, rows_of(b), :] = o_t.T.astype(BF16)
        send_out(0, b)
        gs = gs_buf[b].astype(F32)
        inner = (gs * jnp.concatenate([o_round, o_round], axis=1)).sum(axis=0, keepdims=True)
        inners[b] = jnp.broadcast_to(inner, (8, 2 * BLOCK))
        return c

    def score_grads(b, low, high):
        gs, inner = gs_buf[b], inners[b][0:1, :]
        for j in range(low, high, CHAIN):
            dp = dot(vf[j : j + CHAIN, :], gs)
            ds = e_buf[b, j : j + CHAIN, :].astype(F32) * (dp - inner)
            ds_buf[b, j : j + CHAIN, :] = ds.astype(BF16)

    def query_grads(b):
        both = dot(kt[...], ds_buf[b])
        dq_t = jnp.where(top, both[:, :BLOCK], both[:, BLOCK:]) * HEAD**-0.5
        results[1, rows_of(b), :] = dq_t.T.astype(BF16)
        send_out(1, b)

    def set_grads(which, other, row, size):
        total = jnp.zeros((size, PAIR), F32)
        for b in range(BLOCKS):
            total = total + dot_nt(which[b, row : row + size, :], other[b])
        return total

    def pooled_part(kv, which, other):
        for row in range(0, POOLED, POOLED // 2):
            part = set_grads(which, other, TOKENS + row, POOLED // 2)
            slots[row : row + POOLED // 2, :] = part.astype(BF16)
        for part in range(SPLIT):
            for a in range(1, HIST + 1):
                blocks = range(part * BLOCKS // SPLIT, (part + 1) * BLOCKS // SPLIT)
                by_age(factors[a - 1], slots, back_out.at[kv, a - 1], blocks)
                history(kv, a, part, True).start()

    def own_part(which, other, dst):
        for row in range(0, TOKENS, HALF):
            dst[row : row + HALF, :] = set_grads(which, other, row, HALF)

    spread = pool_matrix(factors, True)

    def finish_set(kv, total):
        for part in range(SPLIT):
            for a in range(1, HIST + 1):
                history(kv, a, part, True).wait_recv()
            for b in range(part * BLOCKS // SPLIT, (part + 1) * BLOCKS // SPLIT):
                pieces = [back_in[kv, a, b * PART : (b + 1) * PART, :] for a in range(HIST)]
                rows = slice(b * BLOCK, (b + 1) * BLOCK)
                added = total[rows, :] + dot(spread, jnp.concatenate(pieces, axis=0))
                results[2 + kv, rows, :] = added.astype(BF16)
                send_out(2 + kv, b)

    pool(0)
    pool(1)
    history_here(0)
    high0 = scores(0, 0)

    def two_blocks(i, high0):
        b = 2 * i
        high1 = scores(b + 1, 1)
        exponents(b, 0, high0)
        high2 = scores(b + 2, 0)
        exponents(b + 1, 1, high1)
        return high2

    high6 = lax.fori_loop(0, BLOCKS // 2 - 1, two_blocks, high0)
    high7 = scores(BLOCKS - 1, 1)
    exponents(BLOCKS - 2, 0, high6)
    exponents(BLOCKS - 1, 1, high7)
    lax.fori_loop(0, BLOCKS, own_output, 0)
    lax.fori_loop(0, BLOCKS, scaled_grads, 0)
    pooled_part(1, e_buf, gs_buf)
    history_here(1)
    lax.fori_loop(0, BLOCKS, attend, 0)

    def old_scores(b, c):
        score_grads(b, TOKENS, KEYS)
        return c

    lax.fori_loop(0, BLOCKS, old_scores, 0)
    pooled_part(0, ds_buf, qs_buf)

    def own_scores(n, c):
        b = turn(n)
        score_grads(b, 0, TOKENS)
        query_grads(b)
        return c

    lax.fori_loop(0, BLOCKS, own_scores, 0)
    own_part(e_buf, gs_buf, dv_sum)
    finish_set(1, dv_sum)
    own_part(ds_buf, qs_buf, dk_sum)
    finish_set(0, dk_sum)

    for n in range(4):
        heads_sent(n)
    for kv in range(2):
        for a in range(1, HIST + 1):
            for part in range(SPLIT):
                history(kv, a, part).wait_send()
                history(kv, a, part, True).wait_send()
    for n in (0, 1, 3, 2):

        def finish(i, c):
            remote, _, here = out_copy(n, i)

            @pl.when(jnp.logical_not(here))
            def _():
                remote.wait_send()

            part = outs[n].at[0, :, pl.ds(pl.multiple_of(i * PAIR, PAIR), PAIR)]
            pltpu.make_async_copy(part, part, out_recv.at[n, i]).wait()
            return c

        lax.fori_loop(0, 8, finish, 0)


def attention(frames, queries, key_rows, value_rows, grad_out, video_of_frame, age_pool):
    vmem, dma = pltpu.VMEM, pltpu.SemaphoreType.DMA
    any_space = pl.BlockSpec(memory_space=pl.ANY)
    smem = pl.BlockSpec(memory_space=pltpu.SMEM)
    return pl.pallas_call(
        functools.partial(kernel, frames),
        out_shape=[jax.ShapeDtypeStruct(queries.shape, BF16)] * 4,
        in_specs=[smem, smem] + [any_space] * 4,
        out_specs=[any_space] * 4,
        scratch_shapes=[
            vmem((TOKENS, PAIR), BF16),
            vmem((TOKENS, PAIR), BF16),
            vmem((KEYS, PAIR), BF16),
            vmem((KEYS, PAIR), BF16),
            vmem((PAIR, KEYS), BF16),
            vmem((PAIR, KEYS), BF16),
            vmem((2, KEYS, 2 * BLOCK), F32),
            vmem((BLOCKS, KEYS, 2 * BLOCK), BF16),
            vmem((BLOCKS, KEYS, 2 * BLOCK), BF16),
            vmem((BLOCKS, PAIR, 2 * BLOCK), BF16),
            vmem((BLOCKS, PAIR, 2 * BLOCK), BF16),
            vmem((BLOCKS, 8, 2 * BLOCK), F32),
            vmem((BLOCKS, 8, 2 * BLOCK), F32),
            vmem((2, HIST, HALF, PAIR), BF16),
            vmem((2, HIST, HALF, PAIR), BF16),
            vmem((2, HIST, HALF, PAIR), BF16),
            vmem((2, HIST, HALF, PAIR), BF16),
            vmem((POOLED, PAIR), BF16),
            vmem((BLOCKS, PAIR, 2 * BLOCK), F32),
            vmem((TOKENS, PAIR), F32),
            vmem((TOKENS, PAIR), F32),
            vmem((4, TOKENS, PAIR), BF16),
            dma((4, 8)),
            dma((4, 8)),
            dma((2, HIST, SPLIT)),
            dma((2, HIST, SPLIT)),
            dma((2, HIST, SPLIT)),
            dma((2, HIST, SPLIT)),
            dma((4, 8)),
            dma((4, 8)),
        ],
        compiler_params=pltpu.CompilerParams(
            collective_id=0, has_side_effects=True, vmem_limit_bytes=VMEM_BYTES
        ),
        cost_estimate=pl.CostEstimate(flops=5 * 2**29, bytes_accessed=2**21, transcendentals=2**22),
        name="attend_frames",
    )(video_of_frame, age_pool, queries, key_rows, value_rows, grad_out)


def deliver_kernel(*refs):
    copies = [pltpu.make_async_copy(refs[n], refs[4 + n], refs[8].at[n]) for n in range(4)]
    for copy in copies:
        copy.start()
    for copy in copies:
        copy.wait()


def deliver(*results):
    any_space = pl.BlockSpec(memory_space=pl.ANY)
    return pl.pallas_call(
        deliver_kernel,
        out_shape=[jax.ShapeDtypeStruct(x.shape, x.dtype) for x in results],
        in_specs=[pl.BlockSpec(memory_space=pltpu.VMEM)] * 4,
        out_specs=[any_space] * 4,
        scratch_shapes=[pltpu.SemaphoreType.DMA((4,))],
        compiler_params=pltpu.CompilerParams(vmem_limit_bytes=VMEM_BYTES),
        name="deliver",
    )(*results)


def on_device(frames, *arrays):
    return tuple(deliver(*attention(frames, *arrays)))


def solution(mesh):
    split = P("frame", "tok", None)
    return jax.shard_map(
        functools.partial(on_device, mesh.shape["frame"]),
        mesh=mesh,
        in_specs=(split,) * 4 + (P(), P()),
        out_specs=(split,) * 4,
        check_vma=False,
    )
```

```python
import functools

import jax
import jax.numpy as jnp
from jax import lax
from jax.experimental import pallas as pl
from jax.experimental.pallas import tpu as pltpu
from jax.sharding import PartitionSpec as P

F32 = jnp.float32
BF16 = jnp.bfloat16
HEAD = 64
HIST = 3
PAIR = 2 * HEAD
BLOCK = 128
TOKENS = 1024
BLOCKS = TOKENS // BLOCK
HALF = TOKENS // 2
POOLED = TOKENS // 2 + TOKENS // 4 + TOKENS // 8
KEYS = TOKENS + POOLED
START = {2: 0, 4: TOKENS // 2, 8: TOKENS // 2 + TOKENS // 4}
CHAIN = 128
VMEM_BYTES = 60 * 2**20
PART = BLOCK // 2
SPLIT = 2
MESH = pl.DeviceIdType.MESH


def dot(a, b):
    return lax.dot_general(a, b, (((1,), (0,)), ((), ())), preferred_element_type=F32)


def dot_nt(a, b):
    return lax.dot_general(a, b, (((1,), (1,)), ((), ())), preferred_element_type=F32)


def pool_matrix(factors, transposed):
    shape = (BLOCK, HIST * PART) if transposed else (HIST * PART, BLOCK)
    row = lax.broadcasted_iota(jnp.int32, shape, 1 if transposed else 0)
    token = lax.broadcasted_iota(jnp.int32, shape, 0 if transposed else 1)
    out = jnp.zeros(shape, F32)
    for a, factor in enumerate(factors):
        share = jnp.where(factor == 2, 0.5, jnp.where(factor == 4, 0.25, 0.125))
        first = (row - a * PART) * factor
        hit = (row >= a * PART) & (row < (a + 1) * PART) & (token >= first) & (token < first + factor)
        out = jnp.where(hit, share, out)
    return out.astype(BF16)


def by_age(factor, slots, dst, blocks):
    for b in blocks:
        two, four, eight = (START[p] + b * (BLOCK // p) for p in (2, 4, 8))
        low = PART // 4
        dst[b * PART : b * PART + low, :] = jnp.where(
            factor == 2,
            slots[two : two + low, :],
            jnp.where(factor == 4, slots[four : four + low, :], slots[eight : eight + low, :]),
        )
        dst[b * PART + low : b * PART + 2 * low, :] = jnp.where(
            factor == 2, slots[two + low : two + 2 * low, :], slots[four + low : four + 2 * low, :]
        )
        dst[b * PART + 2 * low : (b + 1) * PART, :] = slots[two + 2 * low : two + PART, :]


def by_factor(factors, ages, dst, base):
    for factor in (2, 4, 8):
        size = BLOCK // factor
        for b in range(BLOCKS):
            rows = slice(b * PART, b * PART + size)
            start = base + START[factor] + b * size
            dst[start : start + size, :] = jnp.where(
                factors[0] == factor,
                ages[0][rows, :],
                jnp.where(factors[1] == factor, ages[1][rows, :], ages[2][rows, :]),
            )


def kernel(
    frames,
    video,
    age_pool,
    q_in,
    k_in,
    v_in,
    g_in,
    o_out,
    dq_out,
    dk_out,
    dv_out,
    q,
    g,
    kf,
    vf,
    kt,
    vt,
    s_buf,
    e_buf,
    ds_buf,
    qs_buf,
    gs_buf,
    inverses,
    inners,
    pool_out,
    pool_in,
    back_out,
    back_in,
    slots,
    o_own,
    dk_sum,
    dv_sum,
    results,
    in_send,
    in_recv,
    pool_send,
    pool_recv,
    back_send,
    back_recv,
    out_send,
    out_recv,
):
    f = lax.axis_index("frame")
    t = lax.axis_index("tok")
    column, parity = f // 2, f % 2
    z, core = parity * 4 + t // 2, t % 2
    mine = column * 2 + core

    def at(column_, z_, core_):
        return (column_ * 2 + z_ // 4, (z_ % 4) * 2 + core_)

    def frame_at(frame_):
        return at(frame_ // 2, z, frame_ % 2)

    barrier = pltpu.get_barrier_semaphore()

    def greet(i, c):
        place = (z * 2 + core + i) % 16
        pl.semaphore_signal(
            barrier, inc=1, device_id=at(column, place // 2, place % 2), device_id_type=MESH
        )
        return c

    lax.fori_loop(1, 16, greet, 0)
    for a in range(1, HIST + 1):
        for other in ((mine + a) % frames, (mine + frames - a) % frames):
            pl.semaphore_signal(barrier, inc=1, device_id=frame_at(other), device_id_type=MESH)
    pl.semaphore_wait(barrier, 15 + 2 * HIST)

    sources = (k_in, v_in, q_in, g_in)
    arrived = (kf, vf, q, g)
    my_rows = pl.ds(pl.multiple_of(t * BLOCK, BLOCK), BLOCK)

    def rows_of(b):
        return pl.ds(pl.multiple_of(b * BLOCK, BLOCK), BLOCK)

    def head_copy(n, zp):
        src = sources[n].at[0, :, pl.ds(pl.multiple_of(zp * PAIR, PAIR), PAIR)]
        dst = arrived[n].at[my_rows, :]
        there = at(column, zp, parity)
        remote = pltpu.make_async_remote_copy(
            src, dst, in_send.at[n, zp], in_recv.at[n, t], device_id=there, device_id_type=MESH
        )
        local = pltpu.make_async_copy(src, dst, in_recv.at[n, t])
        return remote, local, (zp == z) & (core == parity)

    def send_heads(n):
        def one(i, c):
            remote, local, here = head_copy(n, (z + 12 + (1 - 2 * (i % 2)) * ((i + 1) // 2)) % 8)

            @pl.when(here)
            def _():
                local.start()

            @pl.when(jnp.logical_not(here))
            def _():
                remote.start()

            return c

        lax.fori_loop(0, 8, one, 0)

    def heads_sent(n):
        def one(i, c):
            remote, _, here = head_copy(n, i)

            @pl.when(jnp.logical_not(here))
            def _():
                remote.wait_send()

            return c

        lax.fori_loop(0, 8, one, 0)

    def wait_heads(n, b):
        part = arrived[n].at[rows_of(b), :]
        pltpu.make_async_copy(part, part, in_recv.at[n, b]).wait()

    for n in range(4):
        send_heads(n)

    facing = (z + 4) % 8
    first = jnp.where(facing // 4 == core, facing % 4, 3)

    def nth(n):
        return ((first + 4 - n // 2) % 4) * 2 + n % 2

    factors = [age_pool[a] for a in range(HIST)]
    matrix = pool_matrix(factors, False)
    sets = ((kf, kt), (vf, vt))

    def history(kv, a, part, back=False):
        src, dst, ss, rs = (
            (back_out, back_in, back_send, back_recv) if back else (pool_out, pool_in, pool_send, pool_recv)
        )
        rows = slice(part * HALF // SPLIT, (part + 1) * HALF // SPLIT)
        other = (mine + frames - a) % frames if back else (mine + a) % frames
        return pltpu.make_async_remote_copy(
            src.at[kv, a - 1, rows],
            dst.at[kv, a - 1, rows],
            ss.at[kv, a - 1, part],
            rs.at[kv, a - 1, part],
            device_id=frame_at(other),
            device_id_type=MESH,
        )

    def pool(kv):
        rows, turned = sets[kv]
        for part in range(SPLIT):
            for b in range(part * BLOCKS // SPLIT, (part + 1) * BLOCKS // SPLIT):
                wait_heads(kv, b)
                means = dot(matrix, rows[b * BLOCK : (b + 1) * BLOCK, :]).astype(BF16)
                for a in range(HIST):
                    pool_out[kv, a, b * PART : (b + 1) * PART, :] = means[a * PART : (a + 1) * PART]
            for a in range(1, HIST + 1):
                history(kv, a, part).start()
        turned[:, 0:TOKENS] = rows[0:TOKENS, :].T

    def history_here(kv):
        rows, turned = sets[kv]
        for part in range(SPLIT):
            for a in range(1, HIST + 1):
                history(kv, a, part).wait_recv()
        by_factor(factors, [pool_in.at[kv, a] for a in range(HIST)], rows, TOKENS)
        turned[:, TOKENS:KEYS] = rows[TOKENS:KEYS, :].T

    dead = {}
    for factor in (2, 4, 8):
        bias = jnp.float32(0.0)
        for a in range(1, HIST + 1):
            old = jnp.maximum(mine - a, 0)
            usable = (mine >= a) & (video[old] == video[mine])
            bias = jnp.where((factors[a - 1] == factor) & jnp.logical_not(usable), -1e30, bias)
        dead[factor] = bias

    outs = (o_out, dq_out, dk_out, dv_out)
    my_columns = pl.ds(pl.multiple_of(z * PAIR, PAIR), PAIR)

    def out_copy(n, b):
        src = results.at[n, rows_of(b), :]
        dst = outs[n].at[0, :, my_columns]
        remote = pltpu.make_async_remote_copy(
            src, dst, out_send.at[n, b], out_recv.at[n, z], device_id=(mine, b), device_id_type=MESH
        )
        local = pltpu.make_async_copy(src, dst, out_recv.at[n, z])
        return remote, local, (mine == f) & (b == t)

    def send_out(n, b):
        remote, local, here = out_copy(n, b)

        @pl.when(here)
        def _():
            local.start()

        @pl.when(jnp.logical_not(here))
        def _():
            remote.start()

    top = lax.broadcasted_iota(jnp.int32, (PAIR, BLOCK), 0) < HEAD

    def bias_of(row):
        if row < TOKENS:
            return None
        row -= TOKENS
        return dead[2] if row < START[4] else dead[4] if row < START[8] else dead[8]

    def scores(n, slot):
        b = nth(n)
        q_t = (q[rows_of(b), :].astype(F32) * HEAD**-0.5).T
        qs = jnp.concatenate([jnp.where(top, q_t, 0.0), jnp.where(top, 0.0, q_t)], axis=1).astype(BF16)
        qs_buf[b] = qs
        high = jnp.full((8, 2 * BLOCK), -jnp.inf, F32)
        for j in range(0, KEYS, CHAIN):
            s = dot(kf[j : j + CHAIN, :], qs)
            bias = bias_of(j)
            if bias is not None:
                s = s + bias
            s_buf[slot, j : j + CHAIN, :] = s
            high = jnp.maximum(high, s.reshape(CHAIN // 8, 8, 2 * BLOCK).max(axis=0))
        return high.max(axis=0, keepdims=True)

    def exponents(n, slot, high):
        b = nth(n)
        total = jnp.zeros((8, 2 * BLOCK), F32)
        for j in range(0, KEYS, CHAIN):
            e = jnp.exp(s_buf[slot, j : j + CHAIN, :] - high)
            total = total + e.reshape(CHAIN // 8, 8, 2 * BLOCK).sum(axis=0)
            e_buf[b, j : j + CHAIN, :] = e.astype(BF16)
        inverses[b] = jnp.broadcast_to(1.0 / total.sum(axis=0, keepdims=True), (8, 2 * BLOCK))

    def own_output(i, c):
        for b in (2 * i, 2 * i + 1):
            o_own[b] = dot(vt[:, 0:TOKENS], e_buf[b, 0:TOKENS, :])
        return c

    def scaled_grads(i, c):
        pair = [nth(2 * i), nth(2 * i + 1)]
        for b in pair:
            wait_heads(3, b)
        for b in pair:
            inverse = inverses[b][0:1, :]
            g_t = g[rows_of(b), :].astype(F32).T
            gs_buf[b] = jnp.concatenate(
                [
                    jnp.where(top, g_t, 0.0) * inverse[:, :BLOCK],
                    jnp.where(top, 0.0, g_t) * inverse[:, BLOCK:],
                ],
                axis=1,
            ).astype(BF16)
        return c

    def turn(n):
        return ((z + n // 2) % 4) * 2 + n % 2

    def attend(i, c):
        pair = [turn(2 * i), turn(2 * i + 1)]
        for b in pair:
            both = o_own[b] + dot(vt[:, TOKENS:KEYS], e_buf[b, TOKENS:KEYS, :])
            both = both * inverses[b][0:1, :]
            o_t = jnp.where(top, both[:, :BLOCK], both[:, BLOCK:])
            o_round = o_t.astype(BF16).astype(F32)
            results[0, rows_of(b), :] = o_t.T.astype(BF16)
            gs = gs_buf[b].astype(F32)
            inner = (gs * jnp.concatenate([o_round, o_round], axis=1)).sum(axis=0, keepdims=True)
            inners[b] = jnp.broadcast_to(inner, (8, 2 * BLOCK))
        for b in pair:
            send_out(0, b)
        return c

    def score_grads(b, low, high):
        gs, inner = gs_buf[b], inners[b][0:1, :]
        for j in range(low, high, CHAIN // 2):
            rows = slice(j, j + CHAIN // 2)
            dp = dot(vf[rows, :], gs)
            ds = e_buf[b, rows, :].astype(F32) * (dp - inner)
            ds_buf[b, rows, :] = ds.astype(BF16)

    def query_grads(b):
        both = dot(kt[...], ds_buf[b])
        dq_t = jnp.where(top, both[:, :BLOCK], both[:, BLOCK:]) * HEAD**-0.5
        results[1, rows_of(b), :] = dq_t.T.astype(BF16)

    def set_grads(which, other, row, size):
        total = jnp.zeros((size, PAIR), F32)
        for b in range(BLOCKS):
            total = total + dot_nt(which[b, row : row + size, :], other[b])
        return total

    def pooled_part(kv, which, other):
        slots[...] = set_grads(which, other, TOKENS, POOLED).astype(BF16)
        for part in range(SPLIT):
            for a in range(1, HIST + 1):
                blocks = range(part * BLOCKS // SPLIT, (part + 1) * BLOCKS // SPLIT)
                by_age(factors[a - 1], slots, back_out.at[kv, a - 1], blocks)
                history(kv, a, part, True).start()

    def own_part(which, other, dst):
        dst[...] = set_grads(which, other, 0, TOKENS)

    spread = pool_matrix(factors, True)

    def finish_set(kv, total):
        for part in range(SPLIT):
            for a in range(1, HIST + 1):
                history(kv, a, part, True).wait_recv()
            for b in range(part * BLOCKS // SPLIT, (part + 1) * BLOCKS // SPLIT):
                pieces = [back_in[kv, a, b * PART : (b + 1) * PART, :] for a in range(HIST)]
                rows = slice(b * BLOCK, (b + 1) * BLOCK)
                added = total[rows, :] + dot(spread, jnp.concatenate(pieces, axis=0))
                results[2 + kv, rows, :] = added.astype(BF16)
                send_out(2 + kv, b)

    pool(0)
    pool(1)
    history_here(0)
    wait_heads(2, nth(0))
    high0 = scores(0, 0)

    def two_blocks(i, high0):
        b = 2 * i
        wait_heads(2, nth(b + 1))
        wait_heads(2, nth(b + 2))
        high1 = scores(b + 1, 1)
        exponents(b, 0, high0)
        high2 = scores(b + 2, 0)
        exponents(b + 1, 1, high1)
        return high2

    high6 = lax.fori_loop(0, BLOCKS // 2 - 1, two_blocks, high0)
    wait_heads(2, nth(BLOCKS - 1))
    high7 = scores(BLOCKS - 1, 1)
    exponents(BLOCKS - 2, 0, high6)
    exponents(BLOCKS - 1, 1, high7)
    lax.fori_loop(0, BLOCKS // 2, own_output, 0)
    lax.fori_loop(0, BLOCKS // 2, scaled_grads, 0)
    pooled_part(1, e_buf, gs_buf)
    history_here(1)
    lax.fori_loop(0, BLOCKS // 2, attend, 0)

    def old_scores(i, c):
        for b in (2 * i, 2 * i + 1):
            score_grads(b, TOKENS, KEYS)
        return c

    lax.fori_loop(0, BLOCKS // 2, old_scores, 0)
    pooled_part(0, ds_buf, qs_buf)

    def own_scores(i, c):
        pair = [turn(2 * i), turn(2 * i + 1)]
        for b in pair:
            score_grads(b, 0, TOKENS)
        for b in pair:
            query_grads(b)
        for b in pair:
            send_out(1, b)
        return c

    lax.fori_loop(0, BLOCKS // 2, own_scores, 0)
    own_part(e_buf, gs_buf, dv_sum)
    finish_set(1, dv_sum)
    own_part(ds_buf, qs_buf, dk_sum)
    finish_set(0, dk_sum)

    for n in range(4):
        heads_sent(n)
    for kv in range(2):
        for a in range(1, HIST + 1):
            for part in range(SPLIT):
                history(kv, a, part).wait_send()
                history(kv, a, part, True).wait_send()
    for n in (0, 1, 3, 2):

        def finish(i, c):
            remote, _, here = out_copy(n, i)

            @pl.when(jnp.logical_not(here))
            def _():
                remote.wait_send()

            part = outs[n].at[0, :, pl.ds(pl.multiple_of(i * PAIR, PAIR), PAIR)]
            pltpu.make_async_copy(part, part, out_recv.at[n, i]).wait()
            return c

        lax.fori_loop(0, 8, finish, 0)


def attention(frames, queries, key_rows, value_rows, grad_out, video_of_frame, age_pool):
    vmem, dma = pltpu.VMEM, pltpu.SemaphoreType.DMA
    any_space = pl.BlockSpec(memory_space=pl.ANY)
    smem = pl.BlockSpec(memory_space=pltpu.SMEM)
    return pl.pallas_call(
        functools.partial(kernel, frames),
        out_shape=[jax.ShapeDtypeStruct(queries.shape, BF16)] * 4,
        in_specs=[smem, smem] + [any_space] * 4,
        out_specs=[any_space] * 4,
        scratch_shapes=[
            vmem((TOKENS, PAIR), BF16),
            vmem((TOKENS, PAIR), BF16),
            vmem((KEYS, PAIR), BF16),
            vmem((KEYS, PAIR), BF16),
            vmem((PAIR, KEYS), BF16),
            vmem((PAIR, KEYS), BF16),
            vmem((2, KEYS, 2 * BLOCK), F32),
            vmem((BLOCKS, KEYS, 2 * BLOCK), BF16),
            vmem((BLOCKS, KEYS, 2 * BLOCK), BF16),
            vmem((BLOCKS, PAIR, 2 * BLOCK), BF16),
            vmem((BLOCKS, PAIR, 2 * BLOCK), BF16),
            vmem((BLOCKS, 8, 2 * BLOCK), F32),
            vmem((BLOCKS, 8, 2 * BLOCK), F32),
            vmem((2, HIST, HALF, PAIR), BF16),
            vmem((2, HIST, HALF, PAIR), BF16),
            vmem((2, HIST, HALF, PAIR), BF16),
            vmem((2, HIST, HALF, PAIR), BF16),
            vmem((POOLED, PAIR), BF16),
            vmem((BLOCKS, PAIR, 2 * BLOCK), F32),
            vmem((TOKENS, PAIR), F32),
            vmem((TOKENS, PAIR), F32),
            vmem((4, TOKENS, PAIR), BF16),
            dma((4, 8)),
            dma((4, 8)),
            dma((2, HIST, SPLIT)),
            dma((2, HIST, SPLIT)),
            dma((2, HIST, SPLIT)),
            dma((2, HIST, SPLIT)),
            dma((4, 8)),
            dma((4, 8)),
        ],
        compiler_params=pltpu.CompilerParams(
            collective_id=0, has_side_effects=True, vmem_limit_bytes=VMEM_BYTES
        ),
        cost_estimate=pl.CostEstimate(flops=5 * 2**29, bytes_accessed=2**21, transcendentals=2**22),
        name="attend_frames",
    )(video_of_frame, age_pool, queries, key_rows, value_rows, grad_out)


def deliver_kernel(*refs):
    copies = [pltpu.make_async_copy(refs[n], refs[4 + n], refs[8].at[n]) for n in range(4)]
    for copy in copies:
        copy.start()
    for copy in copies:
        copy.wait()


def deliver(*results):
    any_space = pl.BlockSpec(memory_space=pl.ANY)
    return pl.pallas_call(
        deliver_kernel,
        out_shape=[jax.ShapeDtypeStruct(x.shape, x.dtype) for x in results],
        in_specs=[pl.BlockSpec(memory_space=pltpu.VMEM)] * 4,
        out_specs=[any_space] * 4,
        scratch_shapes=[pltpu.SemaphoreType.DMA((4,))],
        compiler_params=pltpu.CompilerParams(vmem_limit_bytes=VMEM_BYTES),
        name="deliver",
    )(*results)


def on_device(frames, *arrays):
    return tuple(deliver(*attention(frames, *arrays)))


def solution(mesh):
    split = P("frame", "tok", None)
    return jax.shard_map(
        functools.partial(on_device, mesh.shape["frame"]),
        mesh=mesh,
        in_specs=(split,) * 4 + (P(), P()),
        out_specs=(split,) * 4,
        check_vma=False,
    )
```

```python
import functools

import jax
import jax.numpy as jnp
from jax import lax
from jax.experimental import pallas as pl
from jax.experimental.pallas import tpu as pltpu
from jax.sharding import PartitionSpec as P

F32 = jnp.float32
BF16 = jnp.bfloat16
HEAD = 64
HIST = 3
PAIR = 2 * HEAD
BLOCK = 128
TOKENS = 1024
BLOCKS = TOKENS // BLOCK
HALF = TOKENS // 2
POOLED = TOKENS // 2 + TOKENS // 4 + TOKENS // 8
KEYS = TOKENS + POOLED
START = {2: 0, 4: TOKENS // 2, 8: TOKENS // 2 + TOKENS // 4}
CHAIN = 128
VMEM_BYTES = 60 * 2**20
PART = BLOCK // 2
SPLIT = 4
MESH = pl.DeviceIdType.MESH


def dot(a, b):
    return lax.dot_general(a, b, (((1,), (0,)), ((), ())), preferred_element_type=F32)


def dot_nt(a, b):
    return lax.dot_general(a, b, (((1,), (1,)), ((), ())), preferred_element_type=F32)


def pool_matrix(factors, transposed):
    shape = (BLOCK, HIST * PART) if transposed else (HIST * PART, BLOCK)
    row = lax.broadcasted_iota(jnp.int32, shape, 1 if transposed else 0)
    token = lax.broadcasted_iota(jnp.int32, shape, 0 if transposed else 1)
    out = jnp.zeros(shape, F32)
    for a, factor in enumerate(factors):
        share = jnp.where(factor == 2, 0.5, jnp.where(factor == 4, 0.25, 0.125))
        first = (row - a * PART) * factor
        hit = (row >= a * PART) & (row < (a + 1) * PART) & (token >= first) & (token < first + factor)
        out = jnp.where(hit, share, out)
    return out.astype(BF16)


def by_age(factor, slots, dst, blocks):
    for b in blocks:
        two, four, eight = (START[p] + b * (BLOCK // p) for p in (2, 4, 8))
        low = PART // 4
        dst[b * PART : b * PART + low, :] = jnp.where(
            factor == 2,
            slots[two : two + low, :],
            jnp.where(factor == 4, slots[four : four + low, :], slots[eight : eight + low, :]),
        )
        dst[b * PART + low : b * PART + 2 * low, :] = jnp.where(
            factor == 2, slots[two + low : two + 2 * low, :], slots[four + low : four + 2 * low, :]
        )
        dst[b * PART + 2 * low : (b + 1) * PART, :] = slots[two + 2 * low : two + PART, :]


def by_factor(factors, ages, dst, base):
    for factor in (2, 4, 8):
        size = BLOCK // factor
        for b in range(BLOCKS):
            rows = slice(b * PART, b * PART + size)
            start = base + START[factor] + b * size
            dst[start : start + size, :] = jnp.where(
                factors[0] == factor,
                ages[0][rows, :],
                jnp.where(factors[1] == factor, ages[1][rows, :], ages[2][rows, :]),
            )


def kernel(
    frames,
    video,
    age_pool,
    q_in,
    k_in,
    v_in,
    g_in,
    o_out,
    dq_out,
    dk_out,
    dv_out,
    q,
    g,
    kf,
    vf,
    kt,
    vt,
    s_buf,
    e_buf,
    ds_buf,
    qs_buf,
    gs_buf,
    inverses,
    inners,
    pool_out,
    pool_in,
    back_out,
    back_in,
    slots,
    o_own,
    dk_sum,
    dv_sum,
    results,
    in_send,
    in_recv,
    pool_send,
    pool_recv,
    back_send,
    back_recv,
    out_send,
    out_recv,
):
    f = lax.axis_index("frame")
    t = lax.axis_index("tok")
    column, parity = f // 2, f % 2
    z, core = parity * 4 + t // 2, t % 2
    mine = column * 2 + core

    def at(column_, z_, core_):
        return (column_ * 2 + z_ // 4, (z_ % 4) * 2 + core_)

    def frame_at(frame_):
        return at(frame_ // 2, z, frame_ % 2)

    barrier = pltpu.get_barrier_semaphore()

    def greet(i, c):
        place = (z * 2 + core + i) % 16
        pl.semaphore_signal(
            barrier, inc=1, device_id=at(column, place // 2, place % 2), device_id_type=MESH
        )
        return c

    lax.fori_loop(1, 16, greet, 0)
    for a in range(1, HIST + 1):
        for other in ((mine + a) % frames, (mine + frames - a) % frames):
            pl.semaphore_signal(barrier, inc=1, device_id=frame_at(other), device_id_type=MESH)
    pl.semaphore_wait(barrier, 15 + 2 * HIST)

    sources = (k_in, v_in, q_in, g_in)
    arrived = (kf, vf, q, g)
    my_rows = pl.ds(pl.multiple_of(t * BLOCK, BLOCK), BLOCK)

    def rows_of(b):
        return pl.ds(pl.multiple_of(b * BLOCK, BLOCK), BLOCK)

    def head_copy(n, zp):
        src = sources[n].at[0, :, pl.ds(pl.multiple_of(zp * PAIR, PAIR), PAIR)]
        dst = arrived[n].at[my_rows, :]
        there = at(column, zp, parity)
        remote = pltpu.make_async_remote_copy(
            src, dst, in_send.at[n, zp], in_recv.at[n, t], device_id=there, device_id_type=MESH
        )
        local = pltpu.make_async_copy(src, dst, in_recv.at[n, t])
        return remote, local, (zp == z) & (core == parity)

    def send_heads(n):
        def one(i, c):
            remote, local, here = head_copy(n, (z + 12 + (1 - 2 * (i % 2)) * ((i + 1) // 2)) % 8)

            @pl.when(here)
            def _():
                local.start()

            @pl.when(jnp.logical_not(here))
            def _():
                remote.start()

            return c

        lax.fori_loop(0, 8, one, 0)

    def heads_sent(n):
        def one(i, c):
            remote, _, here = head_copy(n, i)

            @pl.when(jnp.logical_not(here))
            def _():
                remote.wait_send()

            return c

        lax.fori_loop(0, 8, one, 0)

    def wait_heads(n, b):
        part = arrived[n].at[rows_of(b), :]
        pltpu.make_async_copy(part, part, in_recv.at[n, b]).wait()

    for n in range(4):
        send_heads(n)

    facing = (z + 4) % 8
    first = jnp.where(facing // 4 == core, facing % 4, 3)

    def nth(n):
        return ((first + 4 - n // 2) % 4) * 2 + n % 2

    factors = [age_pool[a] for a in range(HIST)]
    matrix = pool_matrix(factors, False)
    sets = ((kf, kt), (vf, vt))

    def history(kv, a, part, back=False):
        src, dst, ss, rs = (
            (back_out, back_in, back_send, back_recv) if back else (pool_out, pool_in, pool_send, pool_recv)
        )
        rows = slice(part * HALF // SPLIT, (part + 1) * HALF // SPLIT)
        other = (mine + frames - a) % frames if back else (mine + a) % frames
        return pltpu.make_async_remote_copy(
            src.at[kv, a - 1, rows],
            dst.at[kv, a - 1, rows],
            ss.at[kv, a - 1, part],
            rs.at[kv, a - 1, part],
            device_id=frame_at(other),
            device_id_type=MESH,
        )

    def pool(kv):
        rows, turned = sets[kv]
        for part in range(SPLIT):
            for b in range(part * BLOCKS // SPLIT, (part + 1) * BLOCKS // SPLIT):
                wait_heads(kv, b)
                means = dot(matrix, rows[b * BLOCK : (b + 1) * BLOCK, :]).astype(BF16)
                for a in range(HIST):
                    pool_out[kv, a, b * PART : (b + 1) * PART, :] = means[a * PART : (a + 1) * PART]
            for a in range(1, HIST + 1):
                history(kv, a, part).start()
        turned[:, 0:TOKENS] = rows[0:TOKENS, :].T

    def history_here(kv):
        rows, turned = sets[kv]
        for part in range(SPLIT):
            for a in range(1, HIST + 1):
                history(kv, a, part).wait_recv()
        by_factor(factors, [pool_in.at[kv, a] for a in range(HIST)], rows, TOKENS)
        turned[:, TOKENS:KEYS] = rows[TOKENS:KEYS, :].T

    dead = {}
    for factor in (2, 4, 8):
        bias = jnp.float32(0.0)
        for a in range(1, HIST + 1):
            old = jnp.maximum(mine - a, 0)
            usable = (mine >= a) & (video[old] == video[mine])
            bias = jnp.where((factors[a - 1] == factor) & jnp.logical_not(usable), -1e30, bias)
        dead[factor] = bias

    outs = (o_out, dq_out, dk_out, dv_out)
    my_columns = pl.ds(pl.multiple_of(z * PAIR, PAIR), PAIR)

    def out_copy(n, b):
        src = results.at[n, rows_of(b), :]
        dst = outs[n].at[0, :, my_columns]
        remote = pltpu.make_async_remote_copy(
            src, dst, out_send.at[n, b], out_recv.at[n, z], device_id=(mine, b), device_id_type=MESH
        )
        local = pltpu.make_async_copy(src, dst, out_recv.at[n, z])
        return remote, local, (mine == f) & (b == t)

    def send_out(n, b):
        remote, local, here = out_copy(n, b)

        @pl.when(here)
        def _():
            local.start()

        @pl.when(jnp.logical_not(here))
        def _():
            remote.start()

    top = lax.broadcasted_iota(jnp.int32, (PAIR, BLOCK), 0) < HEAD

    def bias_of(row):
        if row < TOKENS:
            return None
        row -= TOKENS
        return dead[2] if row < START[4] else dead[4] if row < START[8] else dead[8]

    def scores(n, slot):
        b = nth(n)
        q_t = (q[rows_of(b), :].astype(F32) * HEAD**-0.5).T
        qs = jnp.concatenate([jnp.where(top, q_t, 0.0), jnp.where(top, 0.0, q_t)], axis=1).astype(BF16)
        qs_buf[b] = qs
        high = jnp.full((8, 2 * BLOCK), -jnp.inf, F32)
        for j in range(0, KEYS, CHAIN):
            s = dot(kf[j : j + CHAIN, :], qs)
            bias = bias_of(j)
            if bias is not None:
                s = s + bias
            s_buf[slot, j : j + CHAIN, :] = s
            high = jnp.maximum(high, s.reshape(CHAIN // 8, 8, 2 * BLOCK).max(axis=0))
        return high.max(axis=0, keepdims=True)

    def exponents(n, slot, high):
        b = nth(n)
        total = jnp.zeros((8, 2 * BLOCK), F32)
        for j in range(0, KEYS, CHAIN):
            e = jnp.exp(s_buf[slot, j : j + CHAIN, :] - high)
            total = total + e.reshape(CHAIN // 8, 8, 2 * BLOCK).sum(axis=0)
            e_buf[b, j : j + CHAIN, :] = e.astype(BF16)
        inverses[b] = jnp.broadcast_to(1.0 / total.sum(axis=0, keepdims=True), (8, 2 * BLOCK))

    def own_output(i, c):
        for b in (2 * i, 2 * i + 1):
            o_own[b] = dot(vt[:, 0:TOKENS], e_buf[b, 0:TOKENS, :])
        return c

    def scaled_grads(i, c):
        pair = [nth(2 * i), nth(2 * i + 1)]
        for b in pair:
            wait_heads(3, b)
        for b in pair:
            inverse = inverses[b][0:1, :]
            g_t = g[rows_of(b), :].astype(F32).T
            gs_buf[b] = jnp.concatenate(
                [
                    jnp.where(top, g_t, 0.0) * inverse[:, :BLOCK],
                    jnp.where(top, 0.0, g_t) * inverse[:, BLOCK:],
                ],
                axis=1,
            ).astype(BF16)
        return c

    def turn(n):
        return ((z + n // 2) % 4) * 2 + n % 2

    def attend(i, c):
        pair = [turn(2 * i), turn(2 * i + 1)]
        for b in pair:
            both = o_own[b] + dot(vt[:, TOKENS:KEYS], e_buf[b, TOKENS:KEYS, :])
            both = both * inverses[b][0:1, :]
            o_t = jnp.where(top, both[:, :BLOCK], both[:, BLOCK:])
            o_round = o_t.astype(BF16).astype(F32)
            results[0, rows_of(b), :] = o_t.T.astype(BF16)
            gs = gs_buf[b].astype(F32)
            inner = (gs * jnp.concatenate([o_round, o_round], axis=1)).sum(axis=0, keepdims=True)
            inners[b] = jnp.broadcast_to(inner, (8, 2 * BLOCK))
        for b in pair:
            send_out(0, b)
        return c

    def score_grads(b, low, high):
        gs, inner = gs_buf[b], inners[b][0:1, :]
        for j in range(low, high, CHAIN // 2):
            rows = slice(j, j + CHAIN // 2)
            dp = dot(vf[rows, :], gs)
            ds = e_buf[b, rows, :].astype(F32) * (dp - inner)
            ds_buf[b, rows, :] = ds.astype(BF16)

    def query_grads(b):
        both = dot(kt[...], ds_buf[b])
        dq_t = jnp.where(top, both[:, :BLOCK], both[:, BLOCK:]) * HEAD**-0.5
        results[1, rows_of(b), :] = dq_t.T.astype(BF16)

    def set_grads(which, other, row, size):
        total = jnp.zeros((size, PAIR), F32)
        for b in range(BLOCKS):
            total = total + dot_nt(which[b, row : row + size, :], other[b])
        return total

    def pooled_part(kv, which, other):
        slots[...] = set_grads(which, other, TOKENS, POOLED).astype(BF16)
        for part in range(SPLIT):
            for a in range(1, HIST + 1):
                blocks = range(part * BLOCKS // SPLIT, (part + 1) * BLOCKS // SPLIT)
                by_age(factors[a - 1], slots, back_out.at[kv, a - 1], blocks)
                history(kv, a, part, True).start()

    def own_part(which, other, dst):
        dst[...] = set_grads(which, other, 0, TOKENS)

    spread = pool_matrix(factors, True)

    def finish_set(kv, total):
        for part in range(SPLIT):
            for a in range(1, HIST + 1):
                history(kv, a, part, True).wait_recv()
            for b in range(part * BLOCKS // SPLIT, (part + 1) * BLOCKS // SPLIT):
                pieces = [back_in[kv, a, b * PART : (b + 1) * PART, :] for a in range(HIST)]
                rows = slice(b * BLOCK, (b + 1) * BLOCK)
                added = total[rows, :] + dot(spread, jnp.concatenate(pieces, axis=0))
                results[2 + kv, rows, :] = added.astype(BF16)
                send_out(2 + kv, b)

    pool(0)
    pool(1)
    history_here(0)
    wait_heads(2, nth(0))
    high0 = scores(0, 0)

    def two_blocks(i, high0):
        b = 2 * i
        wait_heads(2, nth(b + 1))
        wait_heads(2, nth(b + 2))
        high1 = scores(b + 1, 1)
        exponents(b, 0, high0)
        high2 = scores(b + 2, 0)
        exponents(b + 1, 1, high1)
        return high2

    high6 = lax.fori_loop(0, BLOCKS // 2 - 1, two_blocks, high0)
    wait_heads(2, nth(BLOCKS - 1))
    high7 = scores(BLOCKS - 1, 1)
    exponents(BLOCKS - 2, 0, high6)
    exponents(BLOCKS - 1, 1, high7)
    lax.fori_loop(0, BLOCKS // 2, own_output, 0)
    lax.fori_loop(0, BLOCKS // 2, scaled_grads, 0)
    pooled_part(1, e_buf, gs_buf)
    history_here(1)
    lax.fori_loop(0, BLOCKS // 2, attend, 0)

    def old_scores(i, c):
        for b in (2 * i, 2 * i + 1):
            score_grads(b, TOKENS, KEYS)
        return c

    lax.fori_loop(0, BLOCKS // 2, old_scores, 0)
    pooled_part(0, ds_buf, qs_buf)

    def own_scores(i, c):
        pair = [turn(2 * i), turn(2 * i + 1)]
        for b in pair:
            score_grads(b, 0, TOKENS)
        for b in pair:
            query_grads(b)
        for b in pair:
            send_out(1, b)
        return c

    lax.fori_loop(0, BLOCKS // 2, own_scores, 0)
    own_part(e_buf, gs_buf, dv_sum)
    finish_set(1, dv_sum)
    own_part(ds_buf, qs_buf, dk_sum)
    finish_set(0, dk_sum)

    for n in range(4):
        heads_sent(n)
    for kv in range(2):
        for a in range(1, HIST + 1):
            for part in range(SPLIT):
                history(kv, a, part).wait_send()
                history(kv, a, part, True).wait_send()
    for n in (0, 1, 3, 2):

        def finish(i, c):
            remote, _, here = out_copy(n, i)

            @pl.when(jnp.logical_not(here))
            def _():
                remote.wait_send()

            part = outs[n].at[0, :, pl.ds(pl.multiple_of(i * PAIR, PAIR), PAIR)]
            pltpu.make_async_copy(part, part, out_recv.at[n, i]).wait()
            return c

        lax.fori_loop(0, 8, finish, 0)


def attention(frames, queries, key_rows, value_rows, grad_out, video_of_frame, age_pool):
    vmem, dma = pltpu.VMEM, pltpu.SemaphoreType.DMA
    any_space = pl.BlockSpec(memory_space=pl.ANY)
    smem = pl.BlockSpec(memory_space=pltpu.SMEM)
    return pl.pallas_call(
        functools.partial(kernel, frames),
        out_shape=[jax.ShapeDtypeStruct(queries.shape, BF16)] * 4,
        in_specs=[smem, smem] + [any_space] * 4,
        out_specs=[any_space] * 4,
        scratch_shapes=[
            vmem((TOKENS, PAIR), BF16),
            vmem((TOKENS, PAIR), BF16),
            vmem((KEYS, PAIR), BF16),
            vmem((KEYS, PAIR), BF16),
            vmem((PAIR, KEYS), BF16),
            vmem((PAIR, KEYS), BF16),
            vmem((2, KEYS, 2 * BLOCK), F32),
            vmem((BLOCKS, KEYS, 2 * BLOCK), BF16),
            vmem((BLOCKS, KEYS, 2 * BLOCK), BF16),
            vmem((BLOCKS, PAIR, 2 * BLOCK), BF16),
            vmem((BLOCKS, PAIR, 2 * BLOCK), BF16),
            vmem((BLOCKS, 8, 2 * BLOCK), F32),
            vmem((BLOCKS, 8, 2 * BLOCK), F32),
            vmem((2, HIST, HALF, PAIR), BF16),
            vmem((2, HIST, HALF, PAIR), BF16),
            vmem((2, HIST, HALF, PAIR), BF16),
            vmem((2, HIST, HALF, PAIR), BF16),
            vmem((POOLED, PAIR), BF16),
            vmem((BLOCKS, PAIR, 2 * BLOCK), F32),
            vmem((TOKENS, PAIR), F32),
            vmem((TOKENS, PAIR), F32),
            vmem((4, TOKENS, PAIR), BF16),
            dma((4, 8)),
            dma((4, 8)),
            dma((2, HIST, SPLIT)),
            dma((2, HIST, SPLIT)),
            dma((2, HIST, SPLIT)),
            dma((2, HIST, SPLIT)),
            dma((4, 8)),
            dma((4, 8)),
        ],
        compiler_params=pltpu.CompilerParams(
            collective_id=0, has_side_effects=True, vmem_limit_bytes=VMEM_BYTES
        ),
        cost_estimate=pl.CostEstimate(flops=5 * 2**29, bytes_accessed=2**21, transcendentals=2**22),
        name="attend_frames",
    )(video_of_frame, age_pool, queries, key_rows, value_rows, grad_out)


def deliver_kernel(*refs):
    copies = [pltpu.make_async_copy(refs[n], refs[4 + n], refs[8].at[n]) for n in range(4)]
    for copy in copies:
        copy.start()
    for copy in copies:
        copy.wait()


def deliver(*results):
    any_space = pl.BlockSpec(memory_space=pl.ANY)
    return pl.pallas_call(
        deliver_kernel,
        out_shape=[jax.ShapeDtypeStruct(x.shape, x.dtype) for x in results],
        in_specs=[pl.BlockSpec(memory_space=pltpu.VMEM)] * 4,
        out_specs=[any_space] * 4,
        scratch_shapes=[pltpu.SemaphoreType.DMA((4,))],
        compiler_params=pltpu.CompilerParams(vmem_limit_bytes=VMEM_BYTES),
        name="deliver",
    )(*results)


def on_device(frames, *arrays):
    return tuple(deliver(*attention(frames, *arrays)))


def solution(mesh):
    split = P("frame", "tok", None)
    return jax.shard_map(
        functools.partial(on_device, mesh.shape["frame"]),
        mesh=mesh,
        in_specs=(split,) * 4 + (P(), P()),
        out_specs=(split,) * 4,
        check_vma=False,
    )
```
